32 devices in a mesh: ctx: 4 (over z), fsdp: 8 (over y, x, core).
Axes of the slice: x: 2, y: 2, z: 4, core: 2. Of those that a mesh axis runs over, the one named last changes fastest.
Arguments:
- block_input: bfloat16 [2, 8, 512, 1792], P(None, 'fsdp', 'ctx'), may hold values from -6 to 6
- lengths: int32 [2, 8], P(None, 'fsdp'), may hold values from 128 to 512, as said below
- cotangent: bfloat16 [2, 8, 512, 1792], P(None, 'fsdp', 'ctx'), may hold values from -6 to 6
- gain_attn: bfloat16 [1792], P('fsdp'), may hold values from 0.099609375 to 1.8984375
- conv_taps: bfloat16 [3, 1792], P(None, 'fsdp'), may hold values from -3 to 3
- w_query: bfloat16 [1792, 256], P('fsdp'), may hold values from -0.25 to 0.25
- w_key: bfloat16 [1792, 256], P('fsdp'), may hold values from -0.25 to 0.25
- w_value: bfloat16 [1792, 1792], P('fsdp'), may hold values from -0.125 to 0.125
- w_out: bfloat16 [1792, 1792], P('fsdp'), may hold values from -1 to 1
- gain_ffn: bfloat16 [1792], P('fsdp'), may hold values from 0.099609375 to 1.8984375
- w_gate: bfloat16 [1792, 4864], P('fsdp'), may hold values from -0.125 to 0.125
- w_up: bfloat16 [1792, 4864], P('fsdp'), may hold values from -0.125 to 0.125
- w_down: bfloat16 [4864, 1792], P('fsdp'), may hold values from -0.078125 to 0.078125
Outputs:
- output: bfloat16 [2, 8, 512, 1792], P(None, 'fsdp', 'ctx')
- grad_input: bfloat16 [2, 8, 512, 1792], P(None, 'fsdp', 'ctx')
- grad_gain_attn: float32 [1792], P('fsdp')
- grad_conv_taps: float32 [3, 1792], P(None, 'fsdp')
- grad_w_query: float32 [1792, 256], P('fsdp')
- grad_w_key: float32 [1792, 256], P('fsdp')
- grad_w_value: float32 [1792, 1792], P('fsdp')
- grad_w_out: float32 [1792, 1792], P('fsdp')
- grad_gain_ffn: float32 [1792], P('fsdp')
- grad_w_gate: float32 [1792, 4864], P('fsdp')
- grad_w_up: float32 [1792, 4864], P('fsdp')
- grad_w_down: float32 [4864, 1792], P('fsdp')
The draws below stay inside these ranges and needn't reach their ends.
Inputs may be any that keep to these rules, and one draw needn't show every extreme that they name: `lengths`: for each of the 8 sequence columns, one micro-batch, drawn from the seed, has all 512 slots used.
All inputs are finite; a program needn't handle non-finite values.
Results may differ from the reference program's by a relative error of at most 0.012.
The reference program's roundings to bfloat16 on the way (of `gated`, `mixed`, `normed_two` and `hidden`) count: a program that leaves them out, or rounds other values in their place, can miss the bound.
Values may be sent and summed in bfloat16 or wider, within the bound.
No kernel may reach another device: no remote copies, remote signals or barrier semaphores. Data moves between devices by JAX's collectives and lax.ppermute only.
A program may use at most 384 MiB of HBM per device.

```python
import math
import jax
import jax.numpy as jnp
from jax import lax

D = 1792
HEADS = 16
FEAT = 16
FF = 4864
GROUP = 128
MB = 2
QK = 256
BATCH = 8
LEN = 512


def draw_lengths(key, part):
    key = jax.random.fold_in(key, 11)
    first_key, second_key = jax.random.split(key)
    base = jax.random.randint(first_key, (MB, BATCH), LEN // 4, LEN + 1)
    chosen = jax.random.randint(second_key, (BATCH,), 0, MB)
    rows = jnp.arange(MB, dtype=jnp.int32)[:, None]
    return jnp.where(rows == chosen[None, :], LEN, base).astype(jnp.int32)


def shard_levels(own_key, shape, cuts, least, top_value):
    factor_of, own = 1.0, jax.random.fold_in(own_key, 6)
    for axis_at, shards_of in cuts:
        heights = jnp.exp(jax.random.uniform(jax.random.fold_in(own, axis_at), (shards_of,), jnp.float32, least / len(cuts), top_value / len(cuts)))
        factor_of = factor_of * jnp.repeat(heights, shape[axis_at] // shards_of).reshape([-1 if axis == axis_at else 1 for axis in range(len(shape))])
    return factor_of


def centred(own_key, dims, scale, limit, cuts=(), kind=jnp.bfloat16):
    values = scale * jax.random.normal(own_key, dims, jnp.float32)
    if cuts:
        values = values * shard_levels(own_key, dims, cuts, -0.22, 0.18)
    return jnp.clip(values, -limit, limit).astype(kind)


def setup_inputs(seed: int = 0) -> dict:
    key_list = jax.random.split(jax.random.key(seed), 14)
    block_input = centred(key_list[0], (MB, BATCH, LEN, D), 1.0, 6.0, ((1, 8), (2, 4)))
    lengths = draw_lengths(jax.random.fold_in(key_list[13], 71), 0)
    cotangent = centred(key_list[2], (MB, BATCH, LEN, D), 1.0, 6.0, ((1, 8), (2, 4)))
    gain_attn = jnp.clip(1.0 + 0.18 * jax.random.normal(key_list[3], (D,), jnp.float32), 0.099609375, 1.8984375).astype(jnp.bfloat16)
    conv_taps = centred(key_list[4], (3, D), 0.6, 3.0, ((1, 8),))
    w_query = centred(key_list[5], (D, QK), (D // 4) ** -0.5, 0.25, ((0, 8),))
    w_key = centred(key_list[6], (D, QK), (D // 4) ** -0.5, 0.25, ((0, 8),))
    w_value = centred(key_list[7], (D, D), D ** -0.5, 0.125, ((0, 8),))
    w_out = centred(key_list[8], (D, D), (D // 64) ** -0.5, 1.0, ((0, 8),))
    gain_ffn = jnp.clip(1.0 + 0.18 * jax.random.normal(key_list[9], (D,), jnp.float32), 0.099609375, 1.8984375).astype(jnp.bfloat16)
    w_gate = centred(key_list[10], (D, FF), D ** -0.5, 0.125, ((0, 8),))
    w_up = centred(key_list[11], (D, FF), D ** -0.5, 0.125, ((0, 8),))
    w_down = centred(key_list[12], (FF, D), FF ** -0.5, 0.078125, ((0, 8),))
    return {"block_input": block_input, "lengths": lengths, "cotangent": cotangent, "gain_attn": gain_attn, "conv_taps": conv_taps, "w_query": w_query, "w_key": w_key, "w_value": w_value, "w_out": w_out, "gain_ffn": gain_ffn, "w_gate": w_gate, "w_up": w_up, "w_down": w_down}


@jax.custom_vjp
def low(v):
    return lax.optimization_barrier(v.astype(jnp.bfloat16)).astype(jnp.float32)

@jax.custom_vjp
def low_back(v):
    return v

def low_keep(v):
    return (low(v), None)

def low_pass(kept, grad):
    return (grad,)

def back_keep(v):
    return (v, None)

def back_low(kept, grad):
    return (low(grad),)
low.defvjp(low_keep, low_pass)
low_back.defvjp(back_keep, back_low)
epsilon = 1e-05
highest = lax.Precision.HIGHEST

def feature(values):
    width = values.shape[-1]
    outer = (values[..., :, None] * values[..., None, :]).reshape(values.shape[:-1] + (width * width,))
    return jnp.concatenate([jnp.ones_like(values[..., :1]), values / math.sqrt(math.sqrt(width)), outer / math.sqrt(2.0 * width)], -1)

def product(left, right):
    return jnp.dot(left, right, precision=highest)

def attend(queries, keys, values):
    blocks = queries.shape[0] // GROUP
    head_size = values.shape[-1] // HEADS
    queries = queries.reshape(blocks, GROUP, HEADS, FEAT)
    keys = keys.reshape(blocks, GROUP, HEADS, FEAT)
    values = values.reshape(blocks, GROUP, HEADS, head_size)
    lower = jnp.tril(jnp.ones((GROUP, GROUP), queries.dtype))

    def block(state_pair, pieces):
        states, normals = state_pair
        query_rows, key_rows, value_rows = pieces
        scores = jnp.einsum('thf,shf->hts', query_rows, key_rows, precision=highest) / math.sqrt(FEAT)
        weights = (1.0 + scores + 0.5 * scores * scores) * lower
        numerator = jnp.einsum('hts,shd->thd', weights, value_rows, precision=highest)
        denominator = lax.optimization_barrier(jnp.sum(weights, -1)).T
        query_feat = feature(query_rows)
        key_feat = feature(key_rows)
        numerator = numerator + jnp.einsum('thp,phd->thd', query_feat, states, precision=highest)
        denominator = denominator + jnp.einsum('thp,hp->th', query_feat, normals, precision=highest)
        states = states + jnp.einsum('thp,thd->phd', key_feat, value_rows, precision=highest)
        normals = normals + lax.optimization_barrier(jnp.sum(key_feat, 0))
        return ((states, normals), (numerator / denominator[..., None]).reshape(GROUP, HEADS * head_size))
    phi_count = 1 + FEAT + FEAT * FEAT
    start = (jnp.zeros((phi_count, HEADS, head_size), queries.dtype), jnp.zeros((HEADS, phi_count), queries.dtype))
    unused, mixed = lax.scan(jax.checkpoint(block), start, (queries, keys, values))
    return mixed.reshape(blocks * GROUP, HEADS * head_size)

def sequence(params, row_input, row_keep):
    gain_attn, conv_taps, w_query, w_key, w_value, w_out, gain_ffn, w_gate, w_up, w_down = params
    scale_one = lax.rsqrt(lax.optimization_barrier(jnp.mean(row_input * row_input, -1, keepdims=True)) + epsilon)
    normed = row_input * scale_one * gain_attn
    padded = jnp.concatenate([jnp.zeros_like(normed[:2]), normed], 0)
    conv_out = conv_taps[0] * normed + conv_taps[1] * padded[1:-1] + conv_taps[2] * padded[:-2]
    gated = low(conv_out * jax.nn.silu(normed))
    queries = low_back(low(product(gated, w_query)))
    keys = low_back(low(product(gated, w_key)))
    values = low_back(low(product(gated, w_value)))
    mixed = low_back(low(attend(queries, keys, values)))
    branch = low_back(product(mixed, w_out))
    middle = row_input + row_keep[:, None] * branch
    scale_two = lax.rsqrt(lax.optimization_barrier(jnp.mean(middle * middle, -1, keepdims=True)) + epsilon)
    normed_two = low(middle * scale_two * gain_ffn)
    gate_pre = low_back(product(normed_two, w_gate))
    up_pre = low_back(product(normed_two, w_up))
    hidden = low(jax.nn.silu(gate_pre) * up_pre)
    return middle + row_keep[:, None] * product(hidden, w_down)

def reference(block_input, lengths, cotangent, gain_attn, conv_taps, w_query, w_key, w_value, w_out, gain_ffn, w_gate, w_up, w_down):
    full_shape = block_input.shape
    positions = jnp.arange(LEN, dtype=jnp.int32)
    keeps = (positions[None, None, :] < lengths[:, :, None]).astype(jnp.float32).reshape(MB * BATCH, LEN)
    rows = block_input.astype(jnp.float32).reshape(MB * BATCH, LEN, D)
    params = tuple((weight.astype(jnp.float32) for weight in (gain_attn, conv_taps, w_query, w_key, w_value, w_out, gain_ffn, w_gate, w_up, w_down)))

    def forward(rows_in, params_in):

        def step(unused, pieces):
            return (unused, sequence(params_in, pieces[0], pieces[1]))
        unused, results = lax.scan(jax.checkpoint(step), None, (rows_in, keeps))
        return results
    results, pull = jax.vjp(forward, rows, params)
    start_grad = cotangent.astype(jnp.float32).reshape(MB * BATCH, LEN, D) * keeps[:, :, None]
    grad_rows, grads = pull(start_grad)
    return (results.reshape(full_shape).astype(jnp.bfloat16), grad_rows.reshape(full_shape).astype(jnp.bfloat16), grads[0], grads[1], grads[2], grads[3], grads[4], grads[5], grads[6], grads[7], grads[8], grads[9])
```

```python
import functools
import math

import jax
import jax.numpy as jnp
from jax import lax
from jax.experimental import pallas as pl
from jax.experimental.pallas import tpu as pltpu
from jax.sharding import PartitionSpec as P

HEADS = 16
FEAT = 16
PAIR = 2
FREE = pl.CostEstimate(flops=0, bytes_accessed=0, transcendentals=0)

epsilon = 1e-05
bf16 = jnp.bfloat16
f32 = jnp.float32


def dot(left, right, over):
    return lax.dot_general(left, right, (over, ((), ())), preferred_element_type=f32)


def matmul(left, right):
    return dot(left, right, ((1,), (0,)))


def left_contract(left, right):
    return dot(left, right, ((0,), (0,)))


def right_contract(left, right):
    return dot(left, right, ((1,), (1,)))


def along(value, steps):
    count = lax.axis_size("ctx")
    first, last = (max(0, -steps), min(count, count - steps))
    return lax.ppermute(value, "ctx", [(i, i + steps) for i in range(first, last)])


def rotate(value, steps):
    count = lax.axis_size("ctx")
    return lax.ppermute(value, "ctx", [(i, (i + steps) % count) for i in range(count)])


def across(value, mask):
    count = lax.axis_size("fsdp")
    return lax.ppermute(value, "fsdp", [(i, i ^ mask) for i in range(count)])


def diagonal(value):
    count = lax.axis_size("fsdp")
    return lax.ppermute(value, "fsdp", [(i, i ^ (2 if i & 1 else 4)) for i in range(count)])


def interleaved(own, other):
    return [part for pair in zip(own, other) for part in pair]


def swap(pieces):
    return [across(piece, 1) for piece in pieces]


def chip_exchange(pieces):
    return [across(p, PAIR * k) if k else p for k, p in enumerate(pieces)]


def total(pieces):
    return sum(p.astype(f32) for p in pieces[1:]) + pieces[0].astype(f32)


def join(*values):
    return list(lax.optimization_barrier(values))


def pick(stack, index):
    return lax.dynamic_index_in_dim(stack, index, 0, False)


def placed(pieces, indices):
    buffer = jnp.zeros((len(pieces),) + pieces[0].shape, pieces[0].dtype)
    for piece, index in zip(pieces, indices):
        buffer = lax.dynamic_update_index_in_dim(buffer, piece, index, 0)
    return buffer


def kernel_call(kernel, ids, arrays, outs, scratch=(), anywhere=()):
    whole = pl.BlockSpec(memory_space=pltpu.VMEM)
    specs = [pl.BlockSpec(memory_space=pltpu.SMEM)]
    anyplace = pl.BlockSpec(memory_space=pl.ANY)
    specs += [anyplace if i in anywhere else whole for i in range(len(arrays))]
    return pl.pallas_call(
        kernel,
        out_shape=list(outs),
        in_specs=specs,
        out_specs=[whole] * len(outs),
        scratch_shapes=list(scratch),
        compiler_params=pltpu.CompilerParams(vmem_limit_bytes=48 * 1024 * 1024),
        cost_estimate=FREE,
    )(ids, *arrays)


def fetch_rows(pieces, whole, sems, mine):
    size = pieces[0].shape[0]
    copies = []
    for m, piece in enumerate(pieces):
        start = pl.multiple_of((mine ^ m) * size, 16)
        copies.append(pltpu.make_async_copy(piece, whole.at[pl.ds(start, size)], sems.at[m]))
    for copy in copies:
        copy.start()
    return copies


def tiles(size, step):
    return [slice(at, min(at + step, size)) for at in range(0, size, step)]


def route(value, index, refs):
    for at, ref in enumerate(refs):

        @pl.when(index == at)
        def _(ref=ref):
            ref[...] = value


def ring_step(group, place, count):
    return lax.rem(group + count - place, count)


def project_kernel(count, shards, heads, ids, gated, *rest):
    pieces, outs = rest[:shards], rest[shards : shards + count]
    weight, projected, sems = rest[shards + count :]
    place, mine = ids[0], ids[1]
    for copy in fetch_rows(pieces, weight, sems, mine):
        copy.wait()
    width = weight.shape[1]
    for tile in tiles(width, 256):
        projected[:, tile] = matmul(gated[...], weight[:, tile]).astype(bf16)
    features = heads * FEAT
    all_features = features * count
    part = (width - 2 * all_features) // count
    for group in range(count):
        start = 2 * all_features + part * group
        value = jnp.concatenate(
            [
                projected[:, features * group : features * (group + 1)],
                projected[:, all_features + features * group : all_features + features * (group + 1)],
                projected[:, start : start + part],
            ],
            -1,
        )
        route(value, ring_step(group, place, count), outs)


def project_back_kernel(count, shards, heads, ids, *rest):
    ins, pieces = rest[:count], rest[count : count + shards]
    natural, grad = rest[count + shards : count + shards + 2]
    weight, grouped, sems = rest[count + shards + 2 :]
    place, mine = ids[0], ids[1]
    copies = fetch_rows(pieces, weight, sems, mine)
    features = heads * FEAT
    part = ins[0].shape[1] - 2 * features
    for step in range(count):
        grouped[lax.rem(place + step, count)] = ins[step][...]
    parts = [grouped[g, :, :features] for g in range(count)]
    parts += [grouped[g, :, features : 2 * features] for g in range(count)]
    parts += [grouped[g, :, 2 * features :] for g in range(count)]
    natural[...] = jnp.concatenate(parts, -1)
    for copy in copies:
        copy.wait()
    for tile in tiles(weight.shape[0], 256):
        grad[:, tile] = right_contract(natural[...], weight[tile])


def merge_kernel(count, ids, *rest):
    ins = rest[:count]
    weight, inputs, keep, gain, mixed, middle, normed, grouped, branch = rest[count:]
    place = ids[0]
    for step in range(count):
        grouped[lax.rem(place + step, count)] = ins[step][...]
    mixed[...] = jnp.concatenate([grouped[g] for g in range(count)], -1)
    for tile in tiles(weight.shape[1], 256):
        branch[:, tile] = matmul(mixed[...], weight[:, tile])

    @pl.loop(0, inputs.shape[0] // 16)
    def _(i):
        rows = pl.ds(pl.multiple_of(i * 16, 16), 16)
        value = inputs[rows].astype(f32) + keep[rows] * branch[rows]
        middle[rows] = value
        scale = lax.rsqrt(jnp.mean(value * value, -1, keepdims=True) + epsilon)
        normed[rows] = (value * scale * gain[...]).astype(bf16)


def norm_back_kernel(count, chips, ids, *rest):
    backs = rest[:chips]
    middle, grad_out, keep, gain, weight = rest[chips : chips + 5]
    grad_middle, grad_branch, grad_gain = rest[chips + 5 : chips + 8]
    outs = rest[chips + 8 :]
    place = ids[0]
    grad_gain[...] = jnp.zeros_like(grad_gain)

    @pl.loop(0, middle.shape[0] // 16)
    def _(i):
        rows = pl.ds(pl.multiple_of(i * 16, 16), 16)
        back = backs[0][rows].astype(f32)
        for ref in backs[1:]:
            back = back + ref[rows].astype(f32)
        value = middle[rows]
        scale = lax.rsqrt(jnp.mean(value * value, -1, keepdims=True) + epsilon)
        grad_gain[...] += jnp.sum(back * value * scale, 0, keepdims=True)
        scaled = back * gain[...]
        cube = scale * scale * scale
        grad = (
            grad_out[rows].astype(f32)
            + scale * scaled
            - value * (cube * jnp.mean(scaled * value, -1, keepdims=True))
        )
        grad_middle[rows] = grad
        grad_branch[rows] = (keep[rows] * grad).astype(bf16)

    part = weight.shape[0] // count
    for group in range(count):
        value = right_contract(grad_branch[...], weight[group * part : (group + 1) * part])
        route(value.astype(bf16), ring_step(group, place, count), outs)


def arrange_kernel(shards, ids, *rest):
    pieces, own_down, other_down = rest[:shards], rest[shards], rest[shards + 1]
    gate, up, down, sems = rest[shards + 2 :]
    mine = ids[1]
    size = pieces[0].shape[1]
    copies = []
    for m, piece in enumerate(pieces):
        rows = pl.ds(pl.multiple_of((mine ^ m) * size, 16), size)
        for half, out in enumerate((gate, up)):
            copies.append(pltpu.make_async_copy(piece.at[half], out.at[rows], sems.at[2 * m + half]))
    size = own_down.shape[0]
    core = lax.rem(mine, PAIR)
    for at, piece in enumerate((own_down, other_down)):
        rows = pl.ds(pl.multiple_of((core ^ at) * size, 16), size)
        copies.append(pltpu.make_async_copy(piece, down.at[rows], sems.at[2 * shards + at]))
    for copy in copies:
        copy.start()
    for copy in copies:
        copy.wait()


def pack_kernel(chips, ids, gate, up, out):
    chip = lax.div(ids[1], PAIR)
    part = gate.shape[1] // chips
    for q in range(chips):
        for half, ref in enumerate((gate, up)):
            out[q ^ chip, half] = ref[:, q * part : (q + 1) * part]


def ffn_kernel(chunks, ids, *rest):
    normed = jnp.concatenate([ref[...] for ref in rest[:chunks]], 0)
    grad_out = jnp.concatenate([ref[...] for ref in rest[chunks : 2 * chunks]], 0)
    gate_w, up_w, down_w = rest[2 * chunks : 2 * chunks + 3]
    outs = rest[2 * chunks + 3 : -2]
    gate_all, up_all = rest[-2:]
    size = normed.shape[0] // chunks

    def put(which, tile, value):
        for k in range(chunks):
            outs[4 * k + which][:, tile] = value[k * size : (k + 1) * size].astype(bf16)

    for tile in tiles(gate_w.shape[1], 256):
        gate_pre = matmul(normed, gate_w[:, tile])
        up_pre = matmul(normed, up_w[:, tile])
        grad_hidden = right_contract(grad_out, down_w[tile])
        sig = jax.nn.sigmoid(gate_pre)
        gate_silu = gate_pre * sig
        gate_back = grad_hidden * up_pre * sig * (1.0 + gate_pre * (1.0 - sig))
        gate_back, up_back = gate_back.astype(bf16), (grad_hidden * gate_silu).astype(bf16)
        gate_all[:, tile], up_all[:, tile] = gate_back, up_back
        put(0, tile, gate_silu * up_pre)
        put(1, tile, gate_back)
        put(2, tile, up_back)
    for tile in tiles(gate_w.shape[0], 256):
        value = right_contract(gate_all[...], gate_w[tile])
        put(3, tile, value + right_contract(up_all[...], up_w[tile]))


def down_kernel(chips, ids, *rest):
    hidden, weight, outs = rest[:chips], rest[chips], rest[chips + 1 :]
    for tile in tiles(weight.shape[1], 256):
        for source, out in zip(hidden, outs):
            out[:, tile] = matmul(source[...], weight[:, tile]).astype(bf16)


def finish_kernel(chips, ids, whole, gate, up):
    chip = lax.div(ids[1], PAIR)
    part = whole.shape[-1]
    for q in range(chips):
        for half, out in enumerate((gate, up)):
            out[:, q * part : (q + 1) * part] = whole[q ^ chip, half].astype(f32)


def weight_grad_kernel(blocks, groups, parts, ids, *rest):
    chunks = (len(rest) - 3) // (groups + 1)
    lefts, rights = rest[:chunks], rest[chunks:-3]
    keeps, sends, turned = rest[-3:]
    mine = lax.rem(ids[1], blocks)
    tokens, rows = lefts[0].shape
    size = rows // blocks
    step = size // parts

    @pl.when((pl.program_id(0) == 0) & (pl.program_id(1) == 0) & (pl.program_id(2) == 0))
    def _():
        for k, left in enumerate(lefts):
            for tile in tiles(rows, 128):
                turned[tile, k * tokens : (k + 1) * tokens] = left[:, tile].T

    for g in range(groups):

        @pl.when(pl.program_id(0) == g)
        def _(g=g):
            right = [part[...] for part in rights[g * chunks : (g + 1) * chunks]]
            right = jnp.concatenate(right, 0)
            for at, out in enumerate((keeps, sends)):
                block = mine ^ (PAIR * pl.program_id(1) + at)
                start = pl.multiple_of(block * size + pl.program_id(2) * step, 16)
                out[0, 0] = matmul(turned[pl.ds(start, step)], right).astype(bf16)


def weight_grad(ids, lefts, rights, blocks, parts=1):
    groups, chunks = len(rights), len(lefts)
    tokens, rows = lefts[0].shape
    columns = rights[0][0].shape[1]
    size = rows // blocks
    out = jax.ShapeDtypeStruct((blocks // PAIR, groups, size, columns), bf16)
    arrays = list(lefts) + [part for right in rights for part in right]
    block = pl.BlockSpec((1, 1, size // parts, columns), lambda g, k, j: (k, g, j, 0))
    return pl.pallas_call(
        functools.partial(weight_grad_kernel, blocks, groups, parts),
        out_shape=[out, out],
        grid=(groups, blocks // PAIR, parts),
        in_specs=[pl.BlockSpec(memory_space=pltpu.SMEM)]
        + [pl.BlockSpec(memory_space=pltpu.VMEM)] * len(arrays),
        out_specs=[block] * 2,
        scratch_shapes=[pltpu.VMEM((rows, chunks * tokens), bf16)],
        compiler_params=pltpu.CompilerParams(vmem_limit_bytes=48 * 1024 * 1024),
        cost_estimate=FREE,
    )(ids, *arrays)


def pack_call(ids, w_gate, w_up, chips):
    rows, columns = w_gate.shape
    out = jax.ShapeDtypeStruct((chips, 2, rows, columns // chips), bf16)
    return kernel_call(functools.partial(pack_kernel, chips), ids, [w_gate, w_up], [out])


def arrange(ids, pieces, own_down, other_down, width):
    shards = len(pieces)
    hidden_width = pieces[0].shape[-1]
    shape_of = jax.ShapeDtypeStruct
    anywhere = pl.BlockSpec(memory_space=pl.ANY)
    return pl.pallas_call(
        functools.partial(arrange_kernel, shards),
        out_shape=[shape_of((width, hidden_width), bf16)] * 2
        + [shape_of((PAIR * own_down.shape[0], width), bf16)],
        in_specs=[pl.BlockSpec(memory_space=pltpu.SMEM)] + [anywhere] * (shards + 2),
        out_specs=[pl.BlockSpec(memory_space=pltpu.VMEM)] * 3,
        scratch_shapes=[pltpu.SemaphoreType.DMA((2 * shards + 2,))],
        compiler_params=pltpu.CompilerParams(vmem_limit_bytes=48 * 1024 * 1024),
        cost_estimate=FREE,
    )(ids, *pieces, own_down, other_down)


def causal(place, count, group, block):
    row_block = lax.rem(place + (count - block), count)
    rows = row_block * group + lax.broadcasted_iota(jnp.int32, (group, count * group), 0)
    column = lax.broadcasted_iota(jnp.int32, (group, count * group), 1)
    ordinal, inner = column // group, column % group
    columns = lax.rem(place + (count - ordinal), count) * group + inner
    return rows >= columns


def head_parts(refs, head, heads, head_size):
    features = heads * FEAT
    queries = [r[0][:, head * FEAT : (head + 1) * FEAT] * 0.25 for r in refs]
    keys = [r[0][:, features + head * FEAT : features + (head + 1) * FEAT] for r in refs]
    start = 2 * features + head * head_size
    values = [r[0][:, start : start + head_size] for r in refs]
    return queries, jnp.concatenate(keys, 0), jnp.concatenate(values, 0)


def attend_kernel(count, heads, head_size, place_ref, *refs):
    ins, outs = refs[:count], refs[count:]
    group = ins[0].shape[1]
    place = place_ref[0]
    masks = [causal(place, count, group, block) for block in range(count)]
    mixed = [[] for _ in range(count)]
    for head in range(heads):
        queries, keys, values = head_parts(ins, head, heads, head_size)
        for block in range(count):
            scores = right_contract(queries[block], keys)
            weights = jnp.where(masks[block], 1.0 + scores + 0.5 * scores * scores, 0.0)
            denominator = jnp.sum(weights, -1, keepdims=True)
            numerator = matmul(weights.astype(bf16), values)
            mixed[block].append((numerator / denominator).astype(bf16))
    for block in range(count):
        outs[block][0] = jnp.concatenate(mixed[block], -1)


def attend_back_kernel(count, heads, head_size, place_ref, *refs):
    ins, grads, outs = refs[:count], refs[count : 2 * count], refs[2 * count :]
    group = ins[0].shape[1]
    place = place_ref[0]
    masks = [causal(place, count, group, block) for block in range(count)]
    dqs = [[] for _ in range(count)]
    dks, dvs = [], []
    for head in range(heads):
        queries, keys, values = head_parts(ins, head, heads, head_size)
        key_back = value_back = 0.0
        for block in range(count):
            upstream = grads[block][0][:, head * head_size : (head + 1) * head_size]
            scores = right_contract(queries[block], keys)
            weights = jnp.where(masks[block], 1.0 + scores + 0.5 * scores * scores, 0.0)
            inverse = 1.0 / jnp.sum(weights, -1, keepdims=True)
            weights = weights * inverse
            inner = right_contract(upstream, values)
            shift = jnp.sum(weights * inner, -1, keepdims=True)
            score_back = (inner - shift) * inverse * (1.0 + scores)
            score_back = jnp.where(masks[block], score_back, 0.0).astype(bf16)
            dqs[block].append((0.25 * matmul(score_back, keys)).astype(bf16))
            key_back = key_back + left_contract(queries[block], score_back)
            value_back = value_back + left_contract(upstream, weights.astype(bf16))
        dks.append(key_back.T.astype(bf16))
        dvs.append(value_back.T.astype(bf16))
    for block in range(count):
        rows = slice(block * group, (block + 1) * group)
        parts = dqs[block] + [k[rows] for k in dks] + [v[rows] for v in dvs]
        outs[block][0] = jnp.concatenate(parts, -1)


def block_call(kernel, ids, arrays, out_width):
    count = lax.axis_size("ctx")
    batch, group, _ = arrays[0].shape
    spec = lambda a: pl.BlockSpec((1, group, a.shape[2]), lambda b: (b, 0, 0))
    out = jax.ShapeDtypeStruct((batch, group, out_width), bf16)
    return pl.pallas_call(
        kernel,
        out_shape=[out] * count,
        grid=(batch,),
        in_specs=[pl.BlockSpec(memory_space=pltpu.SMEM)] + [spec(a) for a in arrays],
        out_specs=[spec(out)] * count,
        compiler_params=pltpu.CompilerParams(vmem_limit_bytes=48 * 1024 * 1024),
        cost_estimate=FREE,
    )(ids, *arrays)


def local(
    block_input,
    lengths,
    cotangent,
    gain_attn,
    conv_taps,
    w_query,
    w_key,
    w_value,
    w_out,
    gain_ffn,
    w_gate,
    w_up,
    w_down,
):
    count = lax.axis_size("ctx")
    shards = lax.axis_size("fsdp")
    chips = shards // PAIR
    place = lax.axis_index("ctx")
    mine = lax.axis_index("fsdp")
    core, chip = mine % PAIR, mine // PAIR
    ids = jnp.stack([place, mine]).astype(jnp.int32)
    batch, _, group, width = block_input.shape
    rows = batch * group
    own_rows = w_query.shape[0]
    heads = HEADS // count
    head_size = width // HEADS
    mixed_width = heads * head_size
    qkv_width = 2 * heads * FEAT + mixed_width
    hidden_width = w_gate.shape[1] // chips
    part_rows = own_rows // count
    vmem = lambda shape, kind: pltpu.VMEM(shape, kind)
    shape_of = jax.ShapeDtypeStruct
    rotated = lambda pieces: [rotate(p, d) if d else p for d, p in enumerate(pieces)]
    returned = lambda pieces: [rotate(p, -d) if d else p for d, p in enumerate(pieces)]

    small = jnp.concatenate([gain_attn[None], gain_ffn[None], conv_taps], 0)
    small = jnp.pad(small, ((0, 3), (0, 0)))[None]
    mask = 1
    while mask < shards:
        small = jnp.concatenate([small, across(small, mask)], 0)
        mask *= 2
    small = placed([small[m] for m in range(shards)], [mine ^ m for m in range(shards)])
    small = jnp.transpose(small, (1, 0, 2)).reshape(8, width).astype(f32)
    gain_one, gain_two, taps = small[0], small[1], small[2:5]
    inputs = block_input[:, 0]
    previous = along(inputs[:, group - 2 :], 1)

    qkv_shard = jnp.concatenate([w_query, w_key, w_value], -1)
    total_width = qkv_shard.shape[1]
    if chips == 4:
        one, two = across(qkv_shard, 2), across(qkv_shard, 4)
        (packed,) = pack_call(ids, w_gate, w_up, chips)
        one, two, packed = join(one, two, packed)
        three = diagonal(jnp.where(core == 0, one, two))
        others = swap([qkv_shard, one, two])
        three, *others = join(three, *others)
        qkv_own, qkv_other = [qkv_shard, one, two, three], others + swap([three])
    else:
        (packed,) = pack_call(ids, w_gate, w_up, chips)
        qkv_own = join(*[across(qkv_shard, PAIR * k) if k else qkv_shard for k in range(chips)])
        qkv_other = swap(qkv_own)

    extended = jnp.concatenate([previous, inputs], 1).astype(f32)
    scale_ext = lax.rsqrt(jnp.mean(extended * extended, -1, keepdims=True) + epsilon)
    normed_ext = extended * scale_ext * gain_one
    normed = normed_ext[:, 2:]
    conv_out = taps[0] * normed + taps[1] * normed_ext[:, 1:-1] + taps[2] * normed_ext[:, :-2]
    sig_one = jax.nn.sigmoid(normed)
    gate_act = normed * sig_one
    gated = (conv_out * gate_act).astype(bf16).reshape(rows, width)
    positions = place * group + lax.iota(jnp.int32, group)
    keep = (positions[None] < lengths).astype(f32).reshape(rows, 1)
    grad_out = (cotangent[:, 0].astype(f32).reshape(rows, width) * keep).astype(bf16)

    gated, w_out, w_down, packed, grad_out, *qkv_other = join(
        gated, w_out, w_down, packed, grad_out, *qkv_other
    )
    qkv_pieces = interleaved(qkv_own, qkv_other)
    w_out_full = lax.all_gather(w_out, "fsdp", axis=0, tiled=True)
    columns = [[i + PAIR * k for k in range(chips)] for i in range(PAIR)]
    grad_all = lax.all_gather(grad_out, "fsdp", axis_index_groups=columns)

    projected = kernel_call(
        functools.partial(project_kernel, count, shards, heads),
        ids,
        [gated] + qkv_pieces,
        [shape_of((rows, qkv_width), bf16)] * count,
        scratch=[
            vmem((width, total_width), bf16),
            vmem((rows, total_width), bf16),
            pltpu.SemaphoreType.DMA((shards,)),
        ],
        anywhere=range(1, shards + 1),
    )
    packed, *projected = join(packed, *projected)
    early = max(1, chips - 1)
    gate_up = [across(packed[k], PAIR * k) if k else packed[0] for k in range(early)]
    qkv = rotated(projected)
    qkv = join(*qkv)
    qkv = [a.reshape(batch, group, qkv_width) for a in qkv]
    mixed = block_call(
        functools.partial(attend_kernel, count, heads, head_size), ids, qkv, mixed_width
    )
    *mixed, packed = join(*mixed, packed)
    gate_up += [across(packed[k], PAIR * k) for k in range(early, chips)]
    mixed = returned(mixed)
    both = join(w_down, *gate_up, *mixed)
    own_down, gate_up, mixed = both[0], both[1 : 1 + chips], both[1 + chips :]
    siblings = swap([*gate_up, own_down])
    mixed, middle, normed_two = kernel_call(
        functools.partial(merge_kernel, count),
        ids,
        [a.reshape(rows, mixed_width) for a in mixed]
        + [w_out_full, inputs.reshape(rows, width), keep, gain_two[None]],
        [shape_of((rows, width), kind) for kind in (bf16, f32, bf16)],
        scratch=[vmem((count, rows, mixed_width), bf16), vmem((rows, width), f32)],
    )
    normed_two, other_down, *siblings = join(normed_two, siblings[-1], *siblings[:-1])

    def feed(at, tokens):
        out = [shape_of((rows, hidden_width), bf16)] * 3 + [shape_of((rows, width), bf16)]
        grads = [pick(grad_all, chip ^ k) for k in at]
        outs = kernel_call(
            functools.partial(ffn_kernel, len(at)),
            ids,
            [*tokens, *grads, gate_w, up_w, down_w],
            out * len(at),
            scratch=[vmem((rows * len(at), hidden_width), bf16)] * 2,
        )
        return [[*outs[4 * k : 4 * k + 4], grads[k]] for k in range(len(at))]

    if chips == 4:
        one, two = across(normed_two, 2), across(normed_two, 4)
        gate_w, up_w, down_w = arrange(
            ids, interleaved(gate_up, siblings), w_down, other_down, width
        )
        one, two, gate_w, up_w = join(one, two, gate_w, up_w)
        three = diagonal(jnp.where(core == 0, one, two))
        normed_all = [normed_two, one, two, three]
        last = feed([3], [three])
        last[0][3], one, two = join(last[0][3], one, two)
        received = [across(last[0][3], 6)]
        fed = feed([1, 2], [one, two])
        both = join(normed_two, *received, fed[0][3], fed[1][3])
        normed_own, received, (fed[0][3], fed[1][3]) = both[0], both[1:2], both[2:]
        received += [across(fed[0][3], 2), across(fed[1][3], 4)]
        fed = feed([0], [normed_own]) + fed + last
    else:
        gate_w, up_w, down_w = arrange(
            ids, interleaved(gate_up, siblings), w_down, other_down, width
        )
        normed_all = [across(normed_two, PAIR * k) if k else normed_two for k in range(chips)]
        fed = [feed([k], [normed_all[k]])[0] for k in range(chips)]
        received = [across(fed[k][3], PAIR * k) for k in range(1, chips)]
    hidden_all, gate_back, up_back, backs, grad_all = map(list, zip(*fed))
    down_keeps, down_sends = weight_grad(ids, hidden_all, [grad_all], PAIR, 2)
    both = join(down_sends, gate_back[0], *received)
    down_sends, gate_back[0], received = both[0], both[1], both[2:]

    down_other = across(down_sends[0, 0], 1)
    norm_back = kernel_call(
        functools.partial(norm_back_kernel, count, chips),
        ids,
        [backs[0], *received, middle, grad_out, keep, gain_two[None], w_out_full],
        [shape_of((rows, width), f32), shape_of((rows, width), bf16), shape_of((1, width), f32)]
        + [shape_of((rows, mixed_width), bf16)] * count,
    )
    down_own = (down_keeps[0, 0].astype(f32) + down_other).astype(bf16)
    both = join(down_own, gate_back[0], *norm_back)
    down_own, gate_back[0], norm_back = both[0], both[1], both[2:]
    grad_middle, grad_branch, grad_gain_two = norm_back[:3]

    down_part = lax.psum_scatter(down_own, "ctx", scatter_dimension=0, tiled=True)
    grad_parts = rotated(norm_back[3:])
    keeps, sends = weight_grad(ids, normed_all, [gate_back, up_back], shards)
    out_keeps, out_sends = weight_grad(ids, [mixed], [[grad_branch]], shards)
    downs = kernel_call(
        functools.partial(down_kernel, chips),
        ids,
        hidden_all + [down_w],
        [shape_of((rows, width), bf16)] * chips,
    )
    both = join(sends, out_sends, *grad_parts, *downs)
    sends, out_sends, grad_parts, downs = both[0], both[1], both[2 : 2 + count], both[2 + count :]
    other, out_other = across(sends, 1), across(out_sends[:, 0], 1)
    grad_parts = [a.reshape(batch, group, mixed_width) for a in grad_parts]
    grad_qkv = block_call(
        functools.partial(attend_back_kernel, count, heads, head_size),
        ids,
        qkv + grad_parts,
        qkv_width,
    )
    gate_up_own = [(keeps[k].astype(f32) + other[k]).astype(bf16) for k in range(chips)]
    both = join(down_part, out_other, *grad_qkv, *gate_up_own)
    down_part, out_other, grad_qkv = both[0], both[1], both[2 : 2 + count]
    gate_up_rows = chip_exchange(both[2 + count :])
    grad_qkv = returned(grad_qkv)
    down_whole = lax.all_gather(down_part, "ctx", axis=0, tiled=True)
    both = join(out_other, *grad_qkv, *gate_up_rows[:early])
    out_other, grad_qkv, gate_up_rows[:early] = both[0], both[1 : 1 + count], both[1 + count :]
    grad_qkv, grad_gated = kernel_call(
        functools.partial(project_back_kernel, count, shards, heads),
        ids,
        [a.reshape(rows, qkv_width) for a in grad_qkv] + qkv_pieces,
        [shape_of((rows, total_width), bf16), shape_of((rows, width), f32)],
        scratch=[
            vmem((width, total_width), bf16),
            vmem((count, rows, qkv_width), bf16),
            pltpu.SemaphoreType.DMA((shards,)),
        ],
        anywhere=range(count, count + shards),
    )
    qkv_keeps, qkv_sends = weight_grad(ids, [gated], [[grad_qkv]], shards)
    gate_up_sent = jnp.stack(gate_up_rows).reshape(-1, hidden_width)
    qkv_sends, grad_gated, gate_up_sent = join(qkv_sends, grad_gated, gate_up_sent)

    gate_up_part = lax.psum_scatter(gate_up_sent, "ctx", scatter_dimension=0, tiled=True)
    qkv_other = across(qkv_sends[:, 0], 1)
    out_own = [(out_keeps[k, 0].astype(f32) + out_other[k]).astype(bf16) for k in range(chips)]
    out_rows = chip_exchange(out_own)

    grad_gated = grad_gated.reshape(batch, group, width)
    grad_conv = grad_gated * gate_act
    grad_normed = grad_gated * conv_out * sig_one * (1.0 + normed * (1.0 - sig_one))
    grad_taps = [
        jnp.sum(grad_conv * normed, (0, 1)),
        jnp.sum(grad_conv * normed_ext[:, 1:-1], (0, 1)),
        jnp.sum(grad_conv * normed_ext[:, :-2], (0, 1)),
    ]
    padded = lambda a, before, after: jnp.pad(a, ((0, 0), (before, after), (0, 0)))
    grad_ext = (
        padded(taps[0] * grad_conv, 2, 0)
        + padded(taps[1] * grad_conv, 1, 1)
        + padded(taps[2] * grad_conv, 0, 2)
    )
    later_rows = along(grad_ext[:, :2], -1)
    qkv_own = [(qkv_keeps[k, 0].astype(f32) + qkv_other[k]).astype(bf16) for k in range(chips)]
    grad_normed = grad_normed + grad_ext[:, 2:] + padded(later_rows, group - 2, 0)
    residual = inputs.astype(f32)
    scale_own = scale_ext[:, 2:]
    grad_gain_one = jnp.sum(grad_normed * residual * scale_own, (0, 1))
    scaled_one = grad_normed * gain_one
    cube_one = scale_own * scale_own * scale_own
    grad_rows = (
        grad_middle.reshape(batch, group, width)
        + scale_own * scaled_one
        - residual * cube_one * jnp.mean(scaled_one * residual, -1, keepdims=True)
    ).astype(bf16)
    zero = jnp.zeros_like(grad_gain_one)
    small = jnp.stack([grad_gain_one, grad_gain_two[0]] + grad_taps + [zero, zero, zero])
    small = small + across(small, 1)
    small, grad_rows, *qkv_own = join(small, grad_rows, *qkv_own)
    small = total([small] + [across(small, PAIR * k) for k in range(1, chips)])
    small = lax.dynamic_slice_in_dim(small, mine * own_rows, own_rows, 1).T
    qkv_rows = chip_exchange(qkv_own)

    both = join(gate_up_part, small, *qkv_rows, *out_rows)
    gate_up_part, small, qkv_rows, out_rows = both[0], both[1], both[2 : 2 + chips], both[2 + chips :]
    gate_up_whole = lax.all_gather(gate_up_part, "ctx", axis=0, tiled=True)
    small = jnp.pad(small, ((0, 0), (0, 120)))
    summed = jnp.concatenate([total(qkv_rows), total(out_rows), small], -1).astype(bf16)
    parts = summed.reshape(count, part_rows, summed.shape[1])
    ordered = [(place + step) % count for step in range(count)]
    parts = join(*rotated([pick(parts, at) for at in ordered]))
    part = total(parts).astype(bf16)
    parts = returned([part] * count)
    whole = placed(parts, ordered).reshape(own_rows, summed.shape[1]).astype(f32)
    result = (middle + keep * total(chip_exchange(downs))).astype(bf16)
    gate_up_whole = gate_up_whole.reshape(chips, 2, own_rows, hidden_width)
    grad_w_gate, grad_w_up = kernel_call(
        functools.partial(finish_kernel, chips),
        ids,
        [gate_up_whole],
        [shape_of(w_gate.shape, f32)] * 2,
    )
    small = whole[:, total_width + width :].T
    features = HEADS * FEAT
    return (
        result.reshape(batch, 1, group, width),
        grad_rows[:, None],
        small[0],
        small[2:5],
        whole[:, :features],
        whole[:, features : 2 * features],
        whole[:, 2 * features : total_width],
        whole[:, total_width : total_width + width],
        small[1],
        grad_w_gate,
        grad_w_up,
        down_whole.astype(f32),
    )


def solution(mesh):
    in_specs = (
        P(None, "fsdp", "ctx", None),
        P(None, "fsdp"),
        P(None, "fsdp", "ctx", None),
        P("fsdp"),
        P(None, "fsdp"),
        P("fsdp", None),
        P("fsdp", None),
        P("fsdp", None),
        P("fsdp", None),
        P("fsdp"),
        P("fsdp", None),
        P("fsdp", None),
        P("fsdp", None),
    )
    out_specs = (
        P(None, "fsdp", "ctx", None),
        P(None, "fsdp", "ctx", None),
        P("fsdp"),
        P(None, "fsdp"),
        P("fsdp", None),
        P("fsdp", None),
        P("fsdp", None),
        P("fsdp", None),
        P("fsdp"),
        P("fsdp", None),
        P("fsdp", None),
        P("fsdp", None),
    )
    return jax.shard_map(local, mesh=mesh, in_specs=in_specs, out_specs=out_specs, check_vma=False)
```

```python
import functools
import math

import jax
import jax.numpy as jnp
from jax import lax
from jax.experimental import pallas as pl
from jax.experimental.pallas import tpu as pltpu
from jax.sharding import PartitionSpec as P

HEADS = 16
FEAT = 16
PAIR = 2
FREE = pl.CostEstimate(flops=0, bytes_accessed=0, transcendentals=0)

epsilon = 1e-05
bf16 = jnp.bfloat16
f32 = jnp.float32


def dot(left, right, over):
    return lax.dot_general(left, right, (over, ((), ())), preferred_element_type=f32)


def matmul(left, right):
    return dot(left, right, ((1,), (0,)))


def left_contract(left, right):
    return dot(left, right, ((0,), (0,)))


def right_contract(left, right):
    return dot(left, right, ((1,), (1,)))


def along(value, steps):
    count = lax.axis_size("ctx")
    first, last = (max(0, -steps), min(count, count - steps))
    return lax.ppermute(value, "ctx", [(i, i + steps) for i in range(first, last)])


def rotate(value, steps):
    count = lax.axis_size("ctx")
    return lax.ppermute(value, "ctx", [(i, (i + steps) % count) for i in range(count)])


def across(value, mask):
    count = lax.axis_size("fsdp")
    return lax.ppermute(value, "fsdp", [(i, i ^ mask) for i in range(count)])


def diagonal(value):
    count = lax.axis_size("fsdp")
    return lax.ppermute(value, "fsdp", [(i, i ^ (2 if i & 1 else 4)) for i in range(count)])


def interleaved(own, other):
    return [part for pair in zip(own, other) for part in pair]


def swap(pieces):
    return [across(piece, 1) for piece in pieces]


def chip_exchange(pieces):
    return [across(p, PAIR * k) if k else p for k, p in enumerate(pieces)]


def total(pieces):
    return sum(p.astype(f32) for p in pieces[1:]) + pieces[0].astype(f32)


def join(*values):
    return list(lax.optimization_barrier(values))


def pick(stack, index):
    return lax.dynamic_index_in_dim(stack, index, 0, False)


def placed(pieces, indices):
    buffer = jnp.zeros((len(pieces),) + pieces[0].shape, pieces[0].dtype)
    for piece, index in zip(pieces, indices):
        buffer = lax.dynamic_update_index_in_dim(buffer, piece, index, 0)
    return buffer


def kernel_call(kernel, ids, arrays, outs, scratch=(), anywhere=(), vmem=32):
    whole = pl.BlockSpec(memory_space=pltpu.VMEM)
    specs = [pl.BlockSpec(memory_space=pltpu.SMEM)]
    anyplace = pl.BlockSpec(memory_space=pl.ANY)
    specs += [anyplace if i in anywhere else whole for i in range(len(arrays))]
    return pl.pallas_call(
        kernel,
        out_shape=list(outs),
        in_specs=specs,
        out_specs=[whole] * len(outs),
        scratch_shapes=list(scratch),
        compiler_params=pltpu.CompilerParams(vmem_limit_bytes=vmem * 1024 * 1024),
        cost_estimate=FREE,
    )(ids, *arrays)


def fetch_rows(pieces, whole, sems, mine):
    size = pieces[0].shape[0]
    copies = []
    for m, piece in enumerate(pieces):
        start = pl.multiple_of((mine ^ m) * size, 16)
        copies.append(pltpu.make_async_copy(piece, whole.at[pl.ds(start, size)], sems.at[m]))
    for copy in copies:
        copy.start()
    return copies


def tiles(size, step):
    return [slice(at, min(at + step, size)) for at in range(0, size, step)]


def route(value, index, refs):
    for at, ref in enumerate(refs):

        @pl.when(index == at)
        def _(ref=ref):
            ref[...] = value


def ring_step(group, place, count):
    return lax.rem(group + count - place, count)


def project_kernel(count, shards, heads, ids, gated, *rest):
    pieces, outs = rest[:shards], rest[shards : shards + count]
    weight, projected, sems = rest[shards + count :]
    place, mine = ids[0], ids[1]
    for copy in fetch_rows(pieces, weight, sems, mine):
        copy.wait()
    width = weight.shape[1]
    for tile in tiles(width, 256):
        projected[:, tile] = matmul(gated[...], weight[:, tile]).astype(bf16)
    features = heads * FEAT
    all_features = features * count
    part = (width - 2 * all_features) // count
    for group in range(count):
        start = 2 * all_features + part * group
        value = jnp.concatenate(
            [
                projected[:, features * group : features * (group + 1)],
                projected[:, all_features + features * group : all_features + features * (group + 1)],
                projected[:, start : start + part],
            ],
            -1,
        )
        route(value, ring_step(group, place, count), outs)


def project_back_kernel(count, shards, heads, ids, *rest):
    ins, pieces = rest[:count], rest[count : count + shards]
    natural, grad = rest[count + shards : count + shards + 2]
    weight, grouped, sems = rest[count + shards + 2 :]
    place, mine = ids[0], ids[1]
    copies = fetch_rows(pieces, weight, sems, mine)
    features = heads * FEAT
    part = ins[0].shape[1] - 2 * features
    for step in range(count):
        grouped[lax.rem(place + step, count)] = ins[step][...]
    parts = [grouped[g, :, :features] for g in range(count)]
    parts += [grouped[g, :, features : 2 * features] for g in range(count)]
    parts += [grouped[g, :, 2 * features :] for g in range(count)]
    natural[...] = jnp.concatenate(parts, -1)
    for copy in copies:
        copy.wait()
    for tile in tiles(weight.shape[0], 256):
        grad[:, tile] = right_contract(natural[...], weight[tile])


def merge_kernel(count, ids, *rest):
    ins = rest[:count]
    weight, inputs, keep, gain, mixed, middle, normed, grouped, branch = rest[count:]
    place = ids[0]
    for step in range(count):
        grouped[lax.rem(place + step, count)] = ins[step][...]
    mixed[...] = jnp.concatenate([grouped[g] for g in range(count)], -1)
    for tile in tiles(weight.shape[1], 256):
        branch[:, tile] = matmul(mixed[...], weight[:, tile])

    @pl.loop(0, inputs.shape[0] // 16)
    def _(i):
        rows = pl.ds(pl.multiple_of(i * 16, 16), 16)
        value = inputs[rows].astype(f32) + keep[rows] * branch[rows]
        middle[rows] = value
        scale = lax.rsqrt(jnp.mean(value * value, -1, keepdims=True) + epsilon)
        normed[rows] = (value * scale * gain[...]).astype(bf16)


def norm_back_kernel(count, chips, ids, *rest):
    backs = rest[:chips]
    middle, grad_out, keep, gain, weight = rest[chips : chips + 5]
    grad_middle, grad_branch, grad_gain = rest[chips + 5 : chips + 8]
    outs = rest[chips + 8 :]
    place = ids[0]
    grad_gain[...] = jnp.zeros_like(grad_gain)

    @pl.loop(0, middle.shape[0] // 16)
    def _(i):
        rows = pl.ds(pl.multiple_of(i * 16, 16), 16)
        back = backs[0][rows].astype(f32)
        for ref in backs[1:]:
            back = back + ref[rows].astype(f32)
        value = middle[rows]
        scale = lax.rsqrt(jnp.mean(value * value, -1, keepdims=True) + epsilon)
        grad_gain[...] += jnp.sum(back * value * scale, 0, keepdims=True)
        scaled = back * gain[...]
        cube = scale * scale * scale
        grad = (
            grad_out[rows].astype(f32)
            + scale * scaled
            - value * (cube * jnp.mean(scaled * value, -1, keepdims=True))
        )
        grad_middle[rows] = grad
        grad_branch[rows] = (keep[rows] * grad).astype(bf16)

    part = weight.shape[0] // count
    for group in range(count):
        value = right_contract(grad_branch[...], weight[group * part : (group + 1) * part])
        route(value.astype(bf16), ring_step(group, place, count), outs)


def arrange_kernel(shards, ids, *rest):
    pieces, own_down, other_down = rest[:shards], rest[shards], rest[shards + 1]
    gate, up, down, sems = rest[shards + 2 :]
    mine = ids[1]
    size = pieces[0].shape[1]
    copies = []
    for m, piece in enumerate(pieces):
        rows = pl.ds(pl.multiple_of((mine ^ m) * size, 16), size)
        for half, out in enumerate((gate, up)):
            copies.append(pltpu.make_async_copy(piece.at[half], out.at[rows], sems.at[2 * m + half]))
    size = own_down.shape[0]
    core = lax.rem(mine, PAIR)
    for at, piece in enumerate((own_down, other_down)):
        rows = pl.ds(pl.multiple_of((core ^ at) * size, 16), size)
        copies.append(pltpu.make_async_copy(piece, down.at[rows], sems.at[2 * shards + at]))
    for copy in copies:
        copy.start()
    for copy in copies:
        copy.wait()


def pack_kernel(chips, ids, gate, up, out):
    chip = lax.div(ids[1], PAIR)
    part = gate.shape[1] // chips
    for q in range(chips):
        for half, ref in enumerate((gate, up)):
            out[q ^ chip, half] = ref[:, q * part : (q + 1) * part]


def feed_kernel(chunks, ids, *rest):
    tokens = jnp.concatenate([ref[...] for ref in rest[:chunks]], 0)
    gate_w, up_w = rest[chunks : chunks + 2]
    hidden, to_gate, to_up = (rest[chunks + 2 + i * chunks :][:chunks] for i in range(3))
    size = tokens.shape[0] // chunks

    def put(refs, tile, value):
        for k, ref in enumerate(refs):
            ref[:, tile] = value[k * size : (k + 1) * size].astype(bf16)

    for tile in tiles(gate_w.shape[1], 256):
        gate_pre = matmul(tokens, gate_w[:, tile])
        up_pre = matmul(tokens, up_w[:, tile])
        sig = jax.nn.sigmoid(gate_pre)
        gate_silu = gate_pre * sig
        put(hidden, tile, gate_silu * up_pre)
        put(to_gate, tile, up_pre * sig * (1.0 + gate_pre * (1.0 - sig)))
        put(to_up, tile, gate_silu)


def feed_back_kernel(chunks, ids, *rest):
    grad_out = jnp.concatenate([ref[...] for ref in rest[:chunks]], 0)
    to_gate = jnp.concatenate([ref[...] for ref in rest[chunks : 2 * chunks]], 0)
    to_up = jnp.concatenate([ref[...] for ref in rest[2 * chunks : 3 * chunks]], 0)
    gate_w, up_w, down_w = rest[3 * chunks : 3 * chunks + 3]
    outs = rest[3 * chunks + 3 : -2]
    gate_all, up_all = rest[-2:]
    size = grad_out.shape[0] // chunks

    def put(which, tile, value):
        for k in range(chunks):
            outs[3 * k + which][:, tile] = value[k * size : (k + 1) * size].astype(bf16)

    for tile in tiles(gate_w.shape[1], 256):
        grad_hidden = right_contract(grad_out, down_w[tile])
        gate_back = (grad_hidden * to_gate[:, tile].astype(f32)).astype(bf16)
        up_back = (grad_hidden * to_up[:, tile].astype(f32)).astype(bf16)
        gate_all[:, tile], up_all[:, tile] = gate_back, up_back
        put(0, tile, gate_back)
        put(1, tile, up_back)
    for tile in tiles(gate_w.shape[0], 256):
        value = right_contract(gate_all[...], gate_w[tile])
        put(2, tile, value + right_contract(up_all[...], up_w[tile]))


def down_kernel(chips, ids, *rest):
    hidden, weight, outs = rest[:chips], rest[chips], rest[chips + 1 :]
    for tile in tiles(weight.shape[1], 256):
        for source, out in zip(hidden, outs):
            out[:, tile] = matmul(source[...], weight[:, tile]).astype(bf16)


def finish_kernel(chips, ids, whole, gate, up):
    chip = lax.div(ids[1], PAIR)
    part = whole.shape[-1]
    for q in range(chips):
        for half, out in enumerate((gate, up)):
            out[:, q * part : (q + 1) * part] = whole[q ^ chip, half].astype(f32)


def weight_grad_kernel(blocks, groups, parts, ids, *rest):
    chunks = (len(rest) - 3) // (groups + 1)
    lefts, rights = rest[:chunks], rest[chunks:-3]
    keeps, sends, turned = rest[-3:]
    mine = lax.rem(ids[1], blocks)
    tokens, rows = lefts[0].shape
    size = rows // blocks
    step = size // parts

    @pl.when((pl.program_id(0) == 0) & (pl.program_id(1) == 0) & (pl.program_id(2) == 0))
    def _():
        for k, left in enumerate(lefts):
            for tile in tiles(rows, 128):
                turned[tile, k * tokens : (k + 1) * tokens] = left[:, tile].T

    for g in range(groups):

        @pl.when(pl.program_id(0) == g)
        def _(g=g):
            right = [part[...] for part in rights[g * chunks : (g + 1) * chunks]]
            right = jnp.concatenate(right, 0)
            for at, out in enumerate((keeps, sends)):
                block = mine ^ (PAIR * pl.program_id(1) + at)
                start = pl.multiple_of(block * size + pl.program_id(2) * step, 16)
                out[0, 0] = matmul(turned[pl.ds(start, step)], right).astype(bf16)


def weight_grad(ids, lefts, rights, blocks, parts=1):
    groups, chunks = len(rights), len(lefts)
    tokens, rows = lefts[0].shape
    columns = rights[0][0].shape[1]
    size = rows // blocks
    out = jax.ShapeDtypeStruct((blocks // PAIR, groups, size, columns), bf16)
    arrays = list(lefts) + [part for right in rights for part in right]
    block = pl.BlockSpec((1, 1, size // parts, columns), lambda g, k, j: (k, g, j, 0))
    return pl.pallas_call(
        functools.partial(weight_grad_kernel, blocks, groups, parts),
        out_shape=[out, out],
        grid=(groups, blocks // PAIR, parts),
        in_specs=[pl.BlockSpec(memory_space=pltpu.SMEM)]
        + [pl.BlockSpec(memory_space=pltpu.VMEM)] * len(arrays),
        out_specs=[block] * 2,
        scratch_shapes=[pltpu.VMEM((rows, chunks * tokens), bf16)],
        compiler_params=pltpu.CompilerParams(vmem_limit_bytes=32 * 1024 * 1024),
        cost_estimate=FREE,
    )(ids, *arrays)


def pack_call(ids, w_gate, w_up, chips):
    rows, columns = w_gate.shape
    out = jax.ShapeDtypeStruct((chips, 2, rows, columns // chips), bf16)
    return kernel_call(functools.partial(pack_kernel, chips), ids, [w_gate, w_up], [out])


def arrange(ids, pieces, own_down, other_down, width):
    shards = len(pieces)
    hidden_width = pieces[0].shape[-1]
    shape_of = jax.ShapeDtypeStruct
    anywhere = pl.BlockSpec(memory_space=pl.ANY)
    return pl.pallas_call(
        functools.partial(arrange_kernel, shards),
        out_shape=[shape_of((width, hidden_width), bf16)] * 2
        + [shape_of((PAIR * own_down.shape[0], width), bf16)],
        in_specs=[pl.BlockSpec(memory_space=pltpu.SMEM)] + [anywhere] * (shards + 2),
        out_specs=[pl.BlockSpec(memory_space=pltpu.VMEM)] * 3,
        scratch_shapes=[pltpu.SemaphoreType.DMA((2 * shards + 2,))],
        compiler_params=pltpu.CompilerParams(vmem_limit_bytes=24 * 1024 * 1024),
        cost_estimate=FREE,
    )(ids, *pieces, own_down, other_down)


def causal(place, count, group, block):
    row_block = lax.rem(place + (count - block), count)
    rows = row_block * group + lax.broadcasted_iota(jnp.int32, (group, count * group), 0)
    column = lax.broadcasted_iota(jnp.int32, (group, count * group), 1)
    ordinal, inner = column // group, column % group
    columns = lax.rem(place + (count - ordinal), count) * group + inner
    return rows >= columns


def head_parts(refs, head, heads, head_size):
    features = heads * FEAT
    queries = [r[0][:, head * FEAT : (head + 1) * FEAT] * 0.25 for r in refs]
    keys = [r[0][:, features + head * FEAT : features + (head + 1) * FEAT] for r in refs]
    start = 2 * features + head * head_size
    values = [r[0][:, start : start + head_size] for r in refs]
    return queries, jnp.concatenate(keys, 0), jnp.concatenate(values, 0)


def attend_kernel(count, heads, head_size, place_ref, *refs):
    ins, outs = refs[:count], refs[count:]
    group = ins[0].shape[1]
    place = place_ref[0]
    masks = [causal(place, count, group, block) for block in range(count)]
    mixed = [[] for _ in range(count)]
    for head in range(heads):
        queries, keys, values = head_parts(ins, head, heads, head_size)
        for block in range(count):
            scores = right_contract(queries[block], keys)
            weights = jnp.where(masks[block], 1.0 + scores + 0.5 * scores * scores, 0.0)
            denominator = jnp.sum(weights, -1, keepdims=True)
            numerator = matmul(weights.astype(bf16), values)
            mixed[block].append((numerator / denominator).astype(bf16))
    for block in range(count):
        outs[block][0] = jnp.concatenate(mixed[block], -1)


def attend_back_kernel(count, heads, head_size, place_ref, *refs):
    ins, grads, outs = refs[:count], refs[count : 2 * count], refs[2 * count :]
    group = ins[0].shape[1]
    place = place_ref[0]
    masks = [causal(place, count, group, block) for block in range(count)]
    dqs = [[] for _ in range(count)]
    dks, dvs = [], []
    for head in range(heads):
        queries, keys, values = head_parts(ins, head, heads, head_size)
        key_back = value_back = 0.0
        for block in range(count):
            upstream = grads[block][0][:, head * head_size : (head + 1) * head_size]
            scores = right_contract(queries[block], keys)
            weights = jnp.where(masks[block], 1.0 + scores + 0.5 * scores * scores, 0.0)
            inverse = 1.0 / jnp.sum(weights, -1, keepdims=True)
            weights = weights * inverse
            inner = right_contract(upstream, values)
            shift = jnp.sum(weights * inner, -1, keepdims=True)
            score_back = (inner - shift) * inverse * (1.0 + scores)
            score_back = jnp.where(masks[block], score_back, 0.0).astype(bf16)
            dqs[block].append((0.25 * matmul(score_back, keys)).astype(bf16))
            key_back = key_back + left_contract(queries[block], score_back)
            value_back = value_back + left_contract(upstream, weights.astype(bf16))
        dks.append(key_back.T.astype(bf16))
        dvs.append(value_back.T.astype(bf16))
    for block in range(count):
        rows = slice(block * group, (block + 1) * group)
        parts = dqs[block] + [k[rows] for k in dks] + [v[rows] for v in dvs]
        outs[block][0] = jnp.concatenate(parts, -1)


def block_call(kernel, ids, arrays, out_width):
    count = lax.axis_size("ctx")
    batch, group, _ = arrays[0].shape
    spec = lambda a: pl.BlockSpec((1, group, a.shape[2]), lambda b: (b, 0, 0))
    out = jax.ShapeDtypeStruct((batch, group, out_width), bf16)
    return pl.pallas_call(
        kernel,
        out_shape=[out] * count,
        grid=(batch,),
        in_specs=[pl.BlockSpec(memory_space=pltpu.SMEM)] + [spec(a) for a in arrays],
        out_specs=[spec(out)] * count,
        compiler_params=pltpu.CompilerParams(vmem_limit_bytes=24 * 1024 * 1024),
        cost_estimate=FREE,
    )(ids, *arrays)


def local(
    block_input,
    lengths,
    cotangent,
    gain_attn,
    conv_taps,
    w_query,
    w_key,
    w_value,
    w_out,
    gain_ffn,
    w_gate,
    w_up,
    w_down,
):
    count = lax.axis_size("ctx")
    shards = lax.axis_size("fsdp")
    chips = shards // PAIR
    place = lax.axis_index("ctx")
    mine = lax.axis_index("fsdp")
    core, chip = mine % PAIR, mine // PAIR
    ids = jnp.stack([place, mine]).astype(jnp.int32)
    batch, _, group, width = block_input.shape
    rows = batch * group
    own_rows = w_query.shape[0]
    heads = HEADS // count
    head_size = width // HEADS
    mixed_width = heads * head_size
    qkv_width = 2 * heads * FEAT + mixed_width
    hidden_width = w_gate.shape[1] // chips
    part_rows = own_rows // count
    vmem = lambda shape, kind: pltpu.VMEM(shape, kind)
    shape_of = jax.ShapeDtypeStruct
    rotated = lambda pieces: [rotate(p, d) if d else p for d, p in enumerate(pieces)]
    returned = lambda pieces: [rotate(p, -d) if d else p for d, p in enumerate(pieces)]

    small = jnp.concatenate([gain_attn[None], gain_ffn[None], conv_taps], 0)
    small = jnp.pad(small, ((0, 3), (0, 0)))[None]
    mask = 1
    while mask < shards:
        small = jnp.concatenate([small, across(small, mask)], 0)
        mask *= 2
    small = placed([small[m] for m in range(shards)], [mine ^ m for m in range(shards)])
    small = jnp.transpose(small, (1, 0, 2)).reshape(8, width).astype(f32)
    gain_one, gain_two, taps = small[0], small[1], small[2:5]
    inputs = block_input[:, 0]
    previous = along(inputs[:, group - 2 :], 1)

    qkv_shard = jnp.concatenate([w_query, w_key, w_value], -1)
    total_width = qkv_shard.shape[1]
    if chips == 4:
        one, two = across(qkv_shard, 2), across(qkv_shard, 4)
        (packed,) = pack_call(ids, w_gate, w_up, chips)
        one, two, packed = join(one, two, packed)
        three = diagonal(jnp.where(core == 0, one, two))
        others = swap([qkv_shard, one, two])
        three, *others = join(three, *others)
        qkv_own, qkv_other = [qkv_shard, one, two, three], others + swap([three])
    else:
        (packed,) = pack_call(ids, w_gate, w_up, chips)
        qkv_own = join(*[across(qkv_shard, PAIR * k) if k else qkv_shard for k in range(chips)])
        qkv_other = swap(qkv_own)

    extended = jnp.concatenate([previous, inputs], 1).astype(f32)
    scale_ext = lax.rsqrt(jnp.mean(extended * extended, -1, keepdims=True) + epsilon)
    normed_ext = extended * scale_ext * gain_one
    normed = normed_ext[:, 2:]
    conv_out = taps[0] * normed + taps[1] * normed_ext[:, 1:-1] + taps[2] * normed_ext[:, :-2]
    sig_one = jax.nn.sigmoid(normed)
    gate_act = normed * sig_one
    gated = (conv_out * gate_act).astype(bf16).reshape(rows, width)
    positions = place * group + lax.iota(jnp.int32, group)
    keep = (positions[None] < lengths).astype(f32).reshape(rows, 1)
    grad_out = (cotangent[:, 0].astype(f32).reshape(rows, width) * keep).astype(bf16)

    gated, w_out, w_down, packed, grad_out, *qkv_other = join(
        gated, w_out, w_down, packed, grad_out, *qkv_other
    )
    qkv_pieces = interleaved(qkv_own, qkv_other)
    w_out_full = lax.all_gather(w_out, "fsdp", axis=0, tiled=True)
    columns = [[i + PAIR * k for k in range(chips)] for i in range(PAIR)]
    grad_all = lax.all_gather(grad_out, "fsdp", axis_index_groups=columns)

    projected = kernel_call(
        functools.partial(project_kernel, count, shards, heads),
        ids,
        [gated] + qkv_pieces,
        [shape_of((rows, qkv_width), bf16)] * count,
        scratch=[
            vmem((width, total_width), bf16),
            vmem((rows, total_width), bf16),
            pltpu.SemaphoreType.DMA((shards,)),
        ],
        anywhere=range(1, shards + 1),
    )
    packed, *projected = join(packed, *projected)
    early = max(1, chips - 1)
    gate_up = [across(packed[k], PAIR * k) if k else packed[0] for k in range(early)]
    qkv = rotated(projected)
    qkv = join(*qkv)
    qkv = [a.reshape(batch, group, qkv_width) for a in qkv]
    mixed = block_call(
        functools.partial(attend_kernel, count, heads, head_size), ids, qkv, mixed_width
    )
    *mixed, packed = join(*mixed, packed)
    gate_up += [across(packed[k], PAIR * k) for k in range(early, chips)]
    mixed = returned(mixed)
    both = join(w_down, *gate_up, *mixed)
    own_down, gate_up, mixed = both[0], both[1 : 1 + chips], both[1 + chips :]
    siblings = swap([*gate_up, own_down])
    mixed, middle, normed_two = kernel_call(
        functools.partial(merge_kernel, count),
        ids,
        [a.reshape(rows, mixed_width) for a in mixed]
        + [w_out_full, inputs.reshape(rows, width), keep, gain_two[None]],
        [shape_of((rows, width), kind) for kind in (bf16, f32, bf16)],
        scratch=[vmem((count, rows, mixed_width), bf16), vmem((rows, width), f32)],
    )
    normed_two, other_down, *siblings = join(normed_two, siblings[-1], *siblings[:-1])

    gate_w, up_w, down_w = arrange(
        ids, interleaved(gate_up, siblings), w_down, other_down, width
    )
    if chips == 4:
        one, two = across(normed_two, 2), across(normed_two, 4)
        one, two, gate_w, up_w = join(one, two, gate_w, up_w)
        normed_all = [normed_two, one, two, diagonal(jnp.where(core == 0, one, two))]
    else:
        normed_all = [across(normed_two, PAIR * k) if k else normed_two for k in range(chips)]
    unit = shape_of((rows, hidden_width), bf16)
    fed = kernel_call(
        functools.partial(feed_kernel, chips),
        ids,
        [*normed_all, gate_w, up_w],
        [unit] * 3 * chips,
        vmem=32,
    )
    hidden_all, to_gate, to_up = fed[:chips], fed[chips : 2 * chips], fed[2 * chips :]
    grad_all = [pick(grad_all, chip ^ k) for k in range(chips)]

    def feed_back(at):
        outs = kernel_call(
            functools.partial(feed_back_kernel, len(at)),
            ids,
            [source[k] for source in (grad_all, to_gate, to_up) for k in at]
            + [gate_w, up_w, down_w],
            [unit, unit, shape_of((rows, width), bf16)] * len(at),
            scratch=[vmem((rows * len(at), hidden_width), bf16)] * 2,
            vmem=32,
        )
        return [list(outs[3 * i : 3 * i + 3]) for i in range(len(at))]

    down_keeps, down_sends = weight_grad(ids, hidden_all, [grad_all], PAIR, 2)
    both = join(down_sends, *grad_all)
    down_sends, grad_all = both[0], both[1:]
    down_other = across(down_sends[0, 0], 1)
    if chips == 4:
        last = feed_back([3])
        down_own = (down_keeps[0, 0].astype(f32) + down_other).astype(bf16)
        both = join(down_own, last[0][2], *grad_all)
        down_own, last[0][2], grad_all = both[0], both[1], both[2:]
        down_part = lax.psum_scatter(down_own, "ctx", scatter_dimension=0, tiled=True)
        received = [across(last[0][2], 6)]
        middles = feed_back([1, 2])
        both = join(*received, middles[0][2], middles[1][2], *grad_all)
        received, middles[0][2], middles[1][2], grad_all = both[:1], both[1], both[2], both[3:]
        received += [across(middles[0][2], 2), across(middles[1][2], 4)]
        fed = feed_back([0]) + middles + last
    else:
        fed = [feed_back([k])[0] for k in range(chips)]
        received = [across(fed[k][2], PAIR * k) for k in range(1, chips)]
        down_own = (down_keeps[0, 0].astype(f32) + down_other).astype(bf16)
        down_part = lax.psum_scatter(down_own, "ctx", scatter_dimension=0, tiled=True)
    gate_back, up_back, backs = map(list, zip(*fed))
    keeps, sends = weight_grad(ids, normed_all, [gate_back, up_back], shards)
    down_part, sends, *received = join(down_part, sends, *received)

    other = across(sends, 1)
    down_parts = [down_part, rotate(down_part, -1)]
    norm_back = kernel_call(
        functools.partial(norm_back_kernel, count, chips),
        ids,
        [backs[0], *received, middle, grad_out, keep, gain_two[None], w_out_full],
        [shape_of((rows, width), f32), shape_of((rows, width), bf16), shape_of((1, width), f32)]
        + [shape_of((rows, mixed_width), bf16)] * count,
    )
    both = join(other, *down_parts, *norm_back)
    other, down_parts, norm_back = both[0], both[1:3], both[3:]
    grad_middle, grad_branch, grad_gain_two = norm_back[:3]

    grad_parts = rotated(norm_back[3:])
    gate_up_own = [(keeps[k].astype(f32) + other[k]).astype(bf16) for k in range(chips)]
    out_keeps, out_sends = weight_grad(ids, [mixed], [[grad_branch]], shards)
    out_other = across(out_sends[:, 0], 1)
    out_own = [(out_keeps[k, 0].astype(f32) + out_other[k]).astype(bf16) for k in range(chips)]
    both = join(down_part, *gate_up_own, *out_own, *grad_parts)
    down_part, gate_up_own, both = both[0], both[1 : 1 + chips], both[1 + chips :]
    out_own, grad_parts = both[:chips], both[chips:]
    down_parts += [rotate(down_part, -step) for step in range(2, count - 1)]
    gate_up_rows = chip_exchange(gate_up_own)[:early]
    grad_parts = [a.reshape(batch, group, mixed_width) for a in grad_parts]
    grad_qkv = block_call(
        functools.partial(attend_back_kernel, count, heads, head_size),
        ids,
        qkv + grad_parts,
        qkv_width,
    )
    both = join(down_part, gate_up_own[-1], *gate_up_rows, *grad_qkv, *down_parts)
    down_part, gate_up_own[-1], gate_up_rows, both = *both[:2], both[2 : 2 + early], both[2 + early :]
    grad_qkv, down_parts = both[:count], both[count:]
    gate_up_rows += chip_exchange(gate_up_own)[early:]
    grad_qkv = returned(grad_qkv)
    gate_up_sent = jnp.stack(gate_up_rows).reshape(-1, hidden_width)
    both = join(gate_up_sent, down_part, *out_own, *grad_qkv)
    gate_up_sent, down_part, out_own, grad_qkv = *both[:2], both[2 : 2 + chips], both[2 + chips :]

    gate_up_part = lax.psum_scatter(gate_up_sent, "ctx", scatter_dimension=0, tiled=True)
    down_parts += [rotate(down_part, -step) for step in range(max(2, count - 1), count)]
    out_rows = chip_exchange(out_own)[:early]
    grad_qkv, grad_gated = kernel_call(
        functools.partial(project_back_kernel, count, shards, heads),
        ids,
        [a.reshape(rows, qkv_width) for a in grad_qkv] + qkv_pieces,
        [shape_of((rows, total_width), bf16), shape_of((rows, width), f32)],
        scratch=[
            vmem((width, total_width), bf16),
            vmem((count, rows, qkv_width), bf16),
            pltpu.SemaphoreType.DMA((shards,)),
        ],
        anywhere=range(count, count + shards),
    )
    qkv_keeps, qkv_sends = weight_grad(ids, [gated], [[grad_qkv]], shards)
    both = join(qkv_sends, grad_gated, out_own[-1], down_w, *out_rows)
    qkv_sends, grad_gated, out_own[-1], down_w, out_rows = *both[:4], both[4:]
    out_rows += chip_exchange(out_own)[early:]
    ordered = [(place + step) % count for step in range(count)]
    qkv_other = across(qkv_sends[:, 0], 1)
    grad_gated = grad_gated.reshape(batch, group, width)
    grad_conv = grad_gated * gate_act
    grad_normed = grad_gated * conv_out * sig_one * (1.0 + normed * (1.0 - sig_one))
    grad_taps = [
        jnp.sum(grad_conv * normed, (0, 1)),
        jnp.sum(grad_conv * normed_ext[:, 1:-1], (0, 1)),
        jnp.sum(grad_conv * normed_ext[:, :-2], (0, 1)),
    ]
    padded = lambda a, before, after: jnp.pad(a, ((0, 0), (before, after), (0, 0)))
    grad_ext = (
        padded(taps[0] * grad_conv, 2, 0)
        + padded(taps[1] * grad_conv, 1, 1)
        + padded(taps[2] * grad_conv, 0, 2)
    )
    later_rows = along(grad_ext[:, :2], -1)
    qkv_own = [(qkv_keeps[k, 0].astype(f32) + qkv_other[k]).astype(bf16) for k in range(chips)]
    both = join(later_rows, down_w, *qkv_own, *out_rows)
    later_rows, down_w, qkv_own, out_rows = *both[:2], both[2 : 2 + chips], both[2 + chips :]
    grad_normed = grad_normed + grad_ext[:, 2:] + padded(later_rows, group - 2, 0)
    residual = inputs.astype(f32)
    scale_own = scale_ext[:, 2:]
    grad_gain_one = jnp.sum(grad_normed * residual * scale_own, (0, 1))
    scaled_one = grad_normed * gain_one
    cube_one = scale_own * scale_own * scale_own
    grad_rows = (
        grad_middle.reshape(batch, group, width)
        + scale_own * scaled_one
        - residual * cube_one * jnp.mean(scaled_one * residual, -1, keepdims=True)
    ).astype(bf16)
    zero = jnp.zeros_like(grad_gain_one)
    small = jnp.stack([grad_gain_one, grad_gain_two[0]] + grad_taps + [zero, zero, zero])
    qkv_rows = chip_exchange(qkv_own)
    small = small + across(small, 1)
    out_sum = total(out_rows).astype(bf16).reshape(count, part_rows, width)
    out_parts = rotated([pick(out_sum, at) for at in ordered])

    both = join(gate_up_part, small, *down_parts, *qkv_rows, *out_parts)
    gate_up_part, small, both = both[0], both[1], both[2:]
    down_parts, qkv_rows, out_parts = both[:count], both[count:][:chips], both[count + chips :]
    gate_up_whole = lax.all_gather(gate_up_part, "ctx", axis=0, tiled=True)
    small = total([small] + [across(small, PAIR * k) for k in range(1, chips)])
    small = lax.dynamic_slice_in_dim(small, mine * own_rows, own_rows, 1)
    parts = total(qkv_rows).astype(bf16).reshape(count, part_rows, total_width)
    parts = rotated([pick(parts, at) for at in ordered])
    out_parts = returned([total(out_parts).astype(bf16)] * count)
    down_whole = placed(down_parts, ordered).reshape(w_down.shape)
    both = join(small, total(parts).astype(bf16), down_w, *hidden_all, *out_parts)
    small, part, down_w, both = *both[:3], both[3:]
    hidden_all, out_parts = both[:chips], both[chips:]
    small = total(rotated([small] * count))
    parts = returned([part] * count)
    whole = placed(parts, ordered).reshape(own_rows, total_width).astype(f32)
    grad_wout = placed(out_parts, ordered).reshape(own_rows, width).astype(f32)
    downs = kernel_call(
        functools.partial(down_kernel, chips),
        ids,
        [*hidden_all, down_w],
        [shape_of((rows, width), bf16)] * chips,
    )
    result = (middle + keep * total(chip_exchange(downs))).astype(bf16)
    gate_up_whole = gate_up_whole.reshape(chips, 2, own_rows, hidden_width)
    grad_w_gate, grad_w_up = kernel_call(
        functools.partial(finish_kernel, chips),
        ids,
        [gate_up_whole],
        [shape_of(w_gate.shape, f32)] * 2,
    )
    features = HEADS * FEAT
    return (
        result.reshape(batch, 1, group, width),
        grad_rows[:, None],
        small[0],
        small[2:5],
        whole[:, :features],
        whole[:, features : 2 * features],
        whole[:, 2 * features :],
        grad_wout,
        small[1],
        grad_w_gate,
        grad_w_up,
        down_whole.astype(f32),
    )


def solution(mesh):
    in_specs = (
        P(None, "fsdp", "ctx", None),
        P(None, "fsdp"),
        P(None, "fsdp", "ctx", None),
        P("fsdp"),
        P(None, "fsdp"),
        P("fsdp", None),
        P("fsdp", None),
        P("fsdp", None),
        P("fsdp", None),
        P("fsdp"),
        P("fsdp", None),
        P("fsdp", None),
        P("fsdp", None),
    )
    out_specs = (
        P(None, "fsdp", "ctx", None),
        P(None, "fsdp", "ctx", None),
        P("fsdp"),
        P(None, "fsdp"),
        P("fsdp", None),
        P("fsdp", None),
        P("fsdp", None),
        P("fsdp", None),
        P("fsdp"),
        P("fsdp", None),
        P("fsdp", None),
        P("fsdp", None),
    )
    return jax.shard_map(local, mesh=mesh, in_specs=in_specs, out_specs=out_specs, check_vma=False)
```

```python
import functools
import math

import jax
import jax.numpy as jnp
from jax import lax
from jax.experimental import pallas as pl
from jax.experimental.pallas import tpu as pltpu
from jax.sharding import PartitionSpec as P

HEADS = 16
FEAT = 16
PAIR = 2
FREE = pl.CostEstimate(flops=0, bytes_accessed=0, transcendentals=0)

epsilon = 1e-05
bf16 = jnp.bfloat16
f32 = jnp.float32


def dot(left, right, over):
    return lax.dot_general(left, right, (over, ((), ())), preferred_element_type=f32)


def matmul(left, right):
    return dot(left, right, ((1,), (0,)))


def left_contract(left, right):
    return dot(left, right, ((0,), (0,)))


def right_contract(left, right):
    return dot(left, right, ((1,), (1,)))


def along(value, steps):
    count = lax.axis_size("ctx")
    first, last = (max(0, -steps), min(count, count - steps))
    return lax.ppermute(value, "ctx", [(i, i + steps) for i in range(first, last)])


def rotate(value, steps):
    count = lax.axis_size("ctx")
    return lax.ppermute(value, "ctx", [(i, (i + steps) % count) for i in range(count)])


def across(value, mask):
    count = lax.axis_size("fsdp")
    return lax.ppermute(value, "fsdp", [(i, i ^ mask) for i in range(count)])


def diagonal(value):
    count = lax.axis_size("fsdp")
    return lax.ppermute(value, "fsdp", [(i, i ^ (2 if i & 1 else 4)) for i in range(count)])


def interleaved(own, other):
    return [part for pair in zip(own, other) for part in pair]


def swap(pieces):
    return [across(piece, 1) for piece in pieces]


def chip_exchange(pieces):
    return [across(p, PAIR * k) if k else p for k, p in enumerate(pieces)]


def total(pieces):
    return sum(p.astype(f32) for p in pieces[1:]) + pieces[0].astype(f32)


def join(*values):
    return list(lax.optimization_barrier(values))


def pick(stack, index):
    return lax.dynamic_index_in_dim(stack, index, 0, False)


def placed(pieces, indices):
    buffer = jnp.zeros((len(pieces),) + pieces[0].shape, pieces[0].dtype)
    for piece, index in zip(pieces, indices):
        buffer = lax.dynamic_update_index_in_dim(buffer, piece, index, 0)
    return buffer


def kernel_call(kernel, ids, arrays, outs, scratch=(), anywhere=(), vmem=32):
    whole = pl.BlockSpec(memory_space=pltpu.VMEM)
    specs = [pl.BlockSpec(memory_space=pltpu.SMEM)]
    anyplace = pl.BlockSpec(memory_space=pl.ANY)
    specs += [anyplace if i in anywhere else whole for i in range(len(arrays))]
    return pl.pallas_call(
        kernel,
        out_shape=list(outs),
        in_specs=specs,
        out_specs=[whole] * len(outs),
        scratch_shapes=list(scratch),
        compiler_params=pltpu.CompilerParams(vmem_limit_bytes=vmem * 1024 * 1024),
        cost_estimate=FREE,
    )(ids, *arrays)


def fetch_rows(pieces, whole, sems, mine):
    size = pieces[0].shape[0]
    copies = []
    for m, piece in enumerate(pieces):
        start = pl.multiple_of((mine ^ m) * size, 16)
        copies.append(pltpu.make_async_copy(piece, whole.at[pl.ds(start, size)], sems.at[m]))
    for copy in copies:
        copy.start()
    return copies


def tiles(size, step):
    return [slice(at, min(at + step, size)) for at in range(0, size, step)]


def route(value, index, refs):
    for at, ref in enumerate(refs):

        @pl.when(index == at)
        def _(ref=ref):
            ref[...] = value


def ring_step(group, place, count):
    return lax.rem(group + count - place, count)


def project_kernel(count, shards, heads, ids, gated, *rest):
    pieces, outs = rest[:shards], rest[shards : shards + count]
    weight, projected, sems = rest[shards + count :]
    place, mine = ids[0], ids[1]
    for copy in fetch_rows(pieces, weight, sems, mine):
        copy.wait()
    width = weight.shape[1]
    for tile in tiles(width, 256):
        projected[:, tile] = matmul(gated[...], weight[:, tile]).astype(bf16)
    features = heads * FEAT
    all_features = features * count
    part = (width - 2 * all_features) // count
    for group in range(count):
        start = 2 * all_features + part * group
        value = jnp.concatenate(
            [
                projected[:, features * group : features * (group + 1)],
                projected[:, all_features + features * group : all_features + features * (group + 1)],
                projected[:, start : start + part],
            ],
            -1,
        )
        route(value, ring_step(group, place, count), outs)


def project_back_kernel(count, shards, heads, ids, *rest):
    ins, pieces = rest[:count], rest[count : count + shards]
    natural, grad = rest[count + shards : count + shards + 2]
    weight, grouped, sems = rest[count + shards + 2 :]
    place, mine = ids[0], ids[1]
    copies = fetch_rows(pieces, weight, sems, mine)
    features = heads * FEAT
    part = ins[0].shape[1] - 2 * features
    for step in range(count):
        grouped[lax.rem(place + step, count)] = ins[step][...]
    parts = [grouped[g, :, :features] for g in range(count)]
    parts += [grouped[g, :, features : 2 * features] for g in range(count)]
    parts += [grouped[g, :, 2 * features :] for g in range(count)]
    natural[...] = jnp.concatenate(parts, -1)
    for copy in copies:
        copy.wait()
    for tile in tiles(weight.shape[0], 256):
        grad[:, tile] = right_contract(natural[...], weight[tile])


def merge_kernel(count, ids, *rest):
    ins = rest[:count]
    weight, inputs, keep, gain, mixed, middle, normed, grouped, branch = rest[count:]
    place = ids[0]
    for step in range(count):
        grouped[lax.rem(place + step, count)] = ins[step][...]
    mixed[...] = jnp.concatenate([grouped[g] for g in range(count)], -1)
    for tile in tiles(weight.shape[1], 256):
        branch[:, tile] = matmul(mixed[...], weight[:, tile])

    @pl.loop(0, inputs.shape[0] // 16)
    def _(i):
        rows = pl.ds(pl.multiple_of(i * 16, 16), 16)
        value = inputs[rows].astype(f32) + keep[rows] * branch[rows]
        middle[rows] = value
        scale = lax.rsqrt(jnp.mean(value * value, -1, keepdims=True) + epsilon)
        normed[rows] = (value * scale * gain[...]).astype(bf16)


def norm_back_kernel(count, chips, ids, *rest):
    backs = rest[:chips]
    middle, grad_out, keep, gain, weight = rest[chips : chips + 5]
    grad_middle, grad_branch, grad_gain = rest[chips + 5 : chips + 8]
    outs = rest[chips + 8 :]
    place = ids[0]
    grad_gain[...] = jnp.zeros_like(grad_gain)

    @pl.loop(0, middle.shape[0] // 16)
    def _(i):
        rows = pl.ds(pl.multiple_of(i * 16, 16), 16)
        back = backs[0][rows].astype(f32)
        for ref in backs[1:]:
            back = back + ref[rows].astype(f32)
        value = middle[rows]
        scale = lax.rsqrt(jnp.mean(value * value, -1, keepdims=True) + epsilon)
        grad_gain[...] += jnp.sum(back * value * scale, 0, keepdims=True)
        scaled = back * gain[...]
        cube = scale * scale * scale
        grad = (
            grad_out[rows].astype(f32)
            + scale * scaled
            - value * (cube * jnp.mean(scaled * value, -1, keepdims=True))
        )
        grad_middle[rows] = grad
        grad_branch[rows] = (keep[rows] * grad).astype(bf16)

    part = weight.shape[0] // count
    for group in range(count):
        value = right_contract(grad_branch[...], weight[group * part : (group + 1) * part])
        route(value.astype(bf16), ring_step(group, place, count), outs)


def arrange_kernel(shards, ids, *rest):
    pieces, own_down, other_down = rest[:shards], rest[shards], rest[shards + 1]
    gate, up, down, sems = rest[shards + 2 :]
    mine = ids[1]
    size = pieces[0].shape[1]
    copies = []
    for m, piece in enumerate(pieces):
        rows = pl.ds(pl.multiple_of((mine ^ m) * size, 16), size)
        for half, out in enumerate((gate, up)):
            copies.append(pltpu.make_async_copy(piece.at[half], out.at[rows], sems.at[2 * m + half]))
    size = own_down.shape[0]
    core = lax.rem(mine, PAIR)
    for at, piece in enumerate((own_down, other_down)):
        rows = pl.ds(pl.multiple_of((core ^ at) * size, 16), size)
        copies.append(pltpu.make_async_copy(piece, down.at[rows], sems.at[2 * shards + at]))
    for copy in copies:
        copy.start()
    for copy in copies:
        copy.wait()


def pack_kernel(chips, ids, gate, up, out):
    chip = lax.div(ids[1], PAIR)
    part = gate.shape[1] // chips
    for q in range(chips):
        for half, ref in enumerate((gate, up)):
            out[q ^ chip, half] = ref[:, q * part : (q + 1) * part]


def feed_kernel(chunks, ids, *rest):
    tokens = jnp.concatenate([ref[...] for ref in rest[:chunks]], 0)
    gate_w, up_w = rest[chunks : chunks + 2]
    hidden, to_gate, to_up = (rest[chunks + 2 + i * chunks :][:chunks] for i in range(3))
    size = tokens.shape[0] // chunks

    def put(refs, tile, value):
        for k, ref in enumerate(refs):
            ref[:, tile] = value[k * size : (k + 1) * size].astype(bf16)

    for tile in tiles(gate_w.shape[1], 256):
        gate_pre = matmul(tokens, gate_w[:, tile])
        up_pre = matmul(tokens, up_w[:, tile])
        sig = jax.nn.sigmoid(gate_pre)
        gate_silu = gate_pre * sig
        put(hidden, tile, gate_silu * up_pre)
        put(to_gate, tile, up_pre * sig * (1.0 + gate_pre * (1.0 - sig)))
        put(to_up, tile, gate_silu)


def feed_back_kernel(chunks, ids, *rest):
    grad_out = jnp.concatenate([ref[...] for ref in rest[:chunks]], 0)
    to_gate = jnp.concatenate([ref[...] for ref in rest[chunks : 2 * chunks]], 0)
    to_up = jnp.concatenate([ref[...] for ref in rest[2 * chunks : 3 * chunks]], 0)
    gate_w, up_w, down_w = rest[3 * chunks : 3 * chunks + 3]
    outs = rest[3 * chunks + 3 : -2]
    gate_all, up_all = rest[-2:]
    size = grad_out.shape[0] // chunks

    def put(which, tile, value):
        for k in range(chunks):
            outs[3 * k + which][:, tile] = value[k * size : (k + 1) * size].astype(bf16)

    for tile in tiles(gate_w.shape[1], 256):
        grad_hidden = right_contract(grad_out, down_w[tile])
        gate_back = (grad_hidden * to_gate[:, tile].astype(f32)).astype(bf16)
        up_back = (grad_hidden * to_up[:, tile].astype(f32)).astype(bf16)
        gate_all[:, tile], up_all[:, tile] = gate_back, up_back
        put(0, tile, gate_back)
        put(1, tile, up_back)
    for tile in tiles(gate_w.shape[0], 256):
        value = right_contract(gate_all[...], gate_w[tile])
        put(2, tile, value + right_contract(up_all[...], up_w[tile]))


def down_kernel(chips, ids, *rest):
    hidden, weight, outs = rest[:chips], rest[chips], rest[chips + 1 :]
    for tile in tiles(weight.shape[1], 256):
        for source, out in zip(hidden, outs):
            out[:, tile] = matmul(source[...], weight[:, tile]).astype(bf16)


def finish_kernel(chips, ids, whole, gate, up):
    chip = lax.div(ids[1], PAIR)
    part = whole.shape[-1]
    for q in range(chips):
        for half, out in enumerate((gate, up)):
            out[:, q * part : (q + 1) * part] = whole[q ^ chip, half].astype(f32)


def weight_grad_kernel(blocks, groups, parts, ids, *rest):
    chunks = (len(rest) - 3) // (groups + 1)
    lefts, rights = rest[:chunks], rest[chunks:-3]
    keeps, sends, turned = rest[-3:]
    mine = lax.rem(ids[1], blocks)
    tokens, rows = lefts[0].shape
    size = rows // blocks
    step = size // parts

    @pl.when((pl.program_id(0) == 0) & (pl.program_id(1) == 0) & (pl.program_id(2) == 0))
    def _():
        for k, left in enumerate(lefts):
            for tile in tiles(rows, 128):
                turned[tile, k * tokens : (k + 1) * tokens] = left[:, tile].T

    for g in range(groups):

        @pl.when(pl.program_id(0) == g)
        def _(g=g):
            right = [part[...] for part in rights[g * chunks : (g + 1) * chunks]]
            right = jnp.concatenate(right, 0)
            for at, out in enumerate((keeps, sends)):
                block = mine ^ (PAIR * pl.program_id(1) + at)
                start = pl.multiple_of(block * size + pl.program_id(2) * step, 16)
                out[0, 0] = matmul(turned[pl.ds(start, step)], right).astype(bf16)


def weight_grad(ids, lefts, rights, blocks, parts=1):
    groups, chunks = len(rights), len(lefts)
    tokens, rows = lefts[0].shape
    columns = rights[0][0].shape[1]
    size = rows // blocks
    out = jax.ShapeDtypeStruct((blocks // PAIR, groups, size, columns), bf16)
    arrays = list(lefts) + [part for right in rights for part in right]
    block = pl.BlockSpec((1, 1, size // parts, columns), lambda g, k, j: (k, g, j, 0))
    return pl.pallas_call(
        functools.partial(weight_grad_kernel, blocks, groups, parts),
        out_shape=[out, out],
        grid=(groups, blocks // PAIR, parts),
        in_specs=[pl.BlockSpec(memory_space=pltpu.SMEM)]
        + [pl.BlockSpec(memory_space=pltpu.VMEM)] * len(arrays),
        out_specs=[block] * 2,
        scratch_shapes=[pltpu.VMEM((rows, chunks * tokens), bf16)],
        compiler_params=pltpu.CompilerParams(vmem_limit_bytes=32 * 1024 * 1024),
        cost_estimate=FREE,
    )(ids, *arrays)


def pack_call(ids, w_gate, w_up, chips):
    rows, columns = w_gate.shape
    out = jax.ShapeDtypeStruct((chips, 2, rows, columns // chips), bf16)
    return kernel_call(functools.partial(pack_kernel, chips), ids, [w_gate, w_up], [out])


def arrange(ids, pieces, own_down, other_down, width):
    shards = len(pieces)
    hidden_width = pieces[0].shape[-1]
    shape_of = jax.ShapeDtypeStruct
    anywhere = pl.BlockSpec(memory_space=pl.ANY)
    return pl.pallas_call(
        functools.partial(arrange_kernel, shards),
        out_shape=[shape_of((width, hidden_width), bf16)] * 2
        + [shape_of((PAIR * own_down.shape[0], width), bf16)],
        in_specs=[pl.BlockSpec(memory_space=pltpu.SMEM)] + [anywhere] * (shards + 2),
        out_specs=[pl.BlockSpec(memory_space=pltpu.VMEM)] * 3,
        scratch_shapes=[pltpu.SemaphoreType.DMA((2 * shards + 2,))],
        compiler_params=pltpu.CompilerParams(vmem_limit_bytes=24 * 1024 * 1024),
        cost_estimate=FREE,
    )(ids, *pieces, own_down, other_down)


def causal(place, count, group, block):
    row_block = lax.rem(place + (count - block), count)
    rows = row_block * group + lax.broadcasted_iota(jnp.int32, (group, count * group), 0)
    column = lax.broadcasted_iota(jnp.int32, (group, count * group), 1)
    ordinal, inner = column // group, column % group
    columns = lax.rem(place + (count - ordinal), count) * group + inner
    return rows >= columns


def head_parts(refs, head, heads, head_size):
    features = heads * FEAT
    queries = [r[0][:, head * FEAT : (head + 1) * FEAT] * 0.25 for r in refs]
    keys = [r[0][:, features + head * FEAT : features + (head + 1) * FEAT] for r in refs]
    start = 2 * features + head * head_size
    values = [r[0][:, start : start + head_size] for r in refs]
    return queries, jnp.concatenate(keys, 0), jnp.concatenate(values, 0)


def attend_kernel(count, heads, head_size, place_ref, *refs):
    ins, outs = refs[:count], refs[count:]
    group = ins[0].shape[1]
    place = place_ref[0]
    masks = [causal(place, count, group, block) for block in range(count)]
    mixed = [[] for _ in range(count)]
    for head in range(heads):
        queries, keys, values = head_parts(ins, head, heads, head_size)
        for block in range(count):
            scores = right_contract(queries[block], keys)
            weights = jnp.where(masks[block], 1.0 + scores + 0.5 * scores * scores, 0.0)
            denominator = jnp.sum(weights, -1, keepdims=True)
            numerator = matmul(weights.astype(bf16), values)
            mixed[block].append((numerator / denominator).astype(bf16))
    for block in range(count):
        outs[block][0] = jnp.concatenate(mixed[block], -1)


def attend_back_kernel(count, heads, head_size, place_ref, *refs):
    ins, grads, outs = refs[:count], refs[count : 2 * count], refs[2 * count :]
    group = ins[0].shape[1]
    place = place_ref[0]
    masks = [causal(place, count, group, block) for block in range(count)]
    dqs = [[] for _ in range(count)]
    dks, dvs = [], []
    for head in range(heads):
        queries, keys, values = head_parts(ins, head, heads, head_size)
        key_back = value_back = 0.0
        for block in range(count):
            upstream = grads[block][0][:, head * head_size : (head + 1) * head_size]
            scores = right_contract(queries[block], keys)
            weights = jnp.where(masks[block], 1.0 + scores + 0.5 * scores * scores, 0.0)
            inverse = 1.0 / jnp.sum(weights, -1, keepdims=True)
            weights = weights * inverse
            inner = right_contract(upstream, values)
            shift = jnp.sum(weights * inner, -1, keepdims=True)
            score_back = (inner - shift) * inverse * (1.0 + scores)
            score_back = jnp.where(masks[block], score_back, 0.0).astype(bf16)
            dqs[block].append((0.25 * matmul(score_back, keys)).astype(bf16))
            key_back = key_back + left_contract(queries[block], score_back)
            value_back = value_back + left_contract(upstream, weights.astype(bf16))
        dks.append(key_back.T.astype(bf16))
        dvs.append(value_back.T.astype(bf16))
    for block in range(count):
        rows = slice(block * group, (block + 1) * group)
        parts = dqs[block] + [k[rows] for k in dks] + [v[rows] for v in dvs]
        outs[block][0] = jnp.concatenate(parts, -1)


def block_call(kernel, ids, arrays, out_width):
    count = lax.axis_size("ctx")
    batch, group, _ = arrays[0].shape
    spec = lambda a: pl.BlockSpec((1, group, a.shape[2]), lambda b: (b, 0, 0))
    out = jax.ShapeDtypeStruct((batch, group, out_width), bf16)
    return pl.pallas_call(
        kernel,
        out_shape=[out] * count,
        grid=(batch,),
        in_specs=[pl.BlockSpec(memory_space=pltpu.SMEM)] + [spec(a) for a in arrays],
        out_specs=[spec(out)] * count,
        compiler_params=pltpu.CompilerParams(vmem_limit_bytes=24 * 1024 * 1024),
        cost_estimate=FREE,
    )(ids, *arrays)


def local(
    block_input,
    lengths,
    cotangent,
    gain_attn,
    conv_taps,
    w_query,
    w_key,
    w_value,
    w_out,
    gain_ffn,
    w_gate,
    w_up,
    w_down,
):
    count = lax.axis_size("ctx")
    shards = lax.axis_size("fsdp")
    chips = shards // PAIR
    place = lax.axis_index("ctx")
    mine = lax.axis_index("fsdp")
    core, chip = mine % PAIR, mine // PAIR
    ids = jnp.stack([place, mine]).astype(jnp.int32)
    batch, _, group, width = block_input.shape
    rows = batch * group
    own_rows = w_query.shape[0]
    heads = HEADS // count
    head_size = width // HEADS
    mixed_width = heads * head_size
    qkv_width = 2 * heads * FEAT + mixed_width
    hidden_width = w_gate.shape[1] // chips
    part_rows = own_rows // count
    vmem = lambda shape, kind: pltpu.VMEM(shape, kind)
    shape_of = jax.ShapeDtypeStruct
    rotated = lambda pieces: [rotate(p, d) if d else p for d, p in enumerate(pieces)]
    returned = lambda pieces: [rotate(p, -d) if d else p for d, p in enumerate(pieces)]

    small = jnp.concatenate([gain_attn[None], gain_ffn[None], conv_taps], 0)
    small = jnp.pad(small, ((0, 3), (0, 0)))[None]
    mask = 1
    while mask < shards:
        small = jnp.concatenate([small, across(small, mask)], 0)
        mask *= 2
    small = placed([small[m] for m in range(shards)], [mine ^ m for m in range(shards)])
    small = jnp.transpose(small, (1, 0, 2)).reshape(8, width).astype(f32)
    gain_one, gain_two, taps = small[0], small[1], small[2:5]
    inputs = block_input[:, 0]
    previous = along(inputs[:, group - 2 :], 1)

    qkv_shard = jnp.concatenate([w_query, w_key, w_value], -1)
    total_width = qkv_shard.shape[1]
    if chips == 4:
        one, two = across(qkv_shard, 2), across(qkv_shard, 4)
        (packed,) = pack_call(ids, w_gate, w_up, chips)
        one, two, packed = join(one, two, packed)
        three = diagonal(jnp.where(core == 0, one, two))
        others = swap([qkv_shard, one, two])
        three, *others = join(three, *others)
        qkv_own, qkv_other = [qkv_shard, one, two, three], others + swap([three])
    else:
        (packed,) = pack_call(ids, w_gate, w_up, chips)
        qkv_own = join(*[across(qkv_shard, PAIR * k) if k else qkv_shard for k in range(chips)])
        qkv_other = swap(qkv_own)

    extended = jnp.concatenate([previous, inputs], 1).astype(f32)
    scale_ext = lax.rsqrt(jnp.mean(extended * extended, -1, keepdims=True) + epsilon)
    normed_ext = extended * scale_ext * gain_one
    normed = normed_ext[:, 2:]
    conv_out = taps[0] * normed + taps[1] * normed_ext[:, 1:-1] + taps[2] * normed_ext[:, :-2]
    sig_one = jax.nn.sigmoid(normed)
    gate_act = normed * sig_one
    gated = (conv_out * gate_act).astype(bf16).reshape(rows, width)
    positions = place * group + lax.iota(jnp.int32, group)
    keep = (positions[None] < lengths).astype(f32).reshape(rows, 1)
    grad_out = (cotangent[:, 0].astype(f32).reshape(rows, width) * keep).astype(bf16)

    gated, w_out, w_down, packed, grad_out, *qkv_other = join(
        gated, w_out, w_down, packed, grad_out, *qkv_other
    )
    qkv_pieces = interleaved(qkv_own, qkv_other)
    w_out_full = lax.all_gather(w_out, "fsdp", axis=0, tiled=True)
    if chips == 4:
        grad_all = [grad_out, across(grad_out, 2), across(grad_out, 4)]
    else:
        grad_all = [across(grad_out, PAIR * k) if k else grad_out for k in range(chips)]

    projected = kernel_call(
        functools.partial(project_kernel, count, shards, heads),
        ids,
        [gated] + qkv_pieces,
        [shape_of((rows, qkv_width), bf16)] * count,
        scratch=[
            vmem((width, total_width), bf16),
            vmem((rows, total_width), bf16),
            pltpu.SemaphoreType.DMA((shards,)),
        ],
        anywhere=range(1, shards + 1),
    )
    packed, *projected = join(packed, *projected)
    early = max(1, chips - 1)
    gate_up = [across(packed[k], PAIR * k) if k else packed[0] for k in range(early)]
    qkv = rotated(projected)
    both = join(*qkv, *grad_all)
    qkv, grad_all = both[:count], both[count:]
    qkv = [a.reshape(batch, group, qkv_width) for a in qkv]
    mixed = block_call(
        functools.partial(attend_kernel, count, heads, head_size), ids, qkv, mixed_width
    )
    *mixed, packed = join(*mixed, packed)
    mixed = returned(mixed)
    relayed = jnp.where(core == 0, grad_all[1], grad_all[2]) if chips == 4 else grad_all.pop()
    both = join(w_down, packed, relayed, *gate_up[:early], *mixed)
    own_down, packed, relayed, gate_up, mixed = *both[:3], both[3 : 3 + early], both[3 + early :]
    grad_all.append(diagonal(relayed) if chips == 4 else relayed)
    siblings = swap([own_down, *gate_up])
    gate_up += [across(packed[k], PAIR * k) for k in range(early, chips)]
    mixed, middle, normed_two = kernel_call(
        functools.partial(merge_kernel, count),
        ids,
        [a.reshape(rows, mixed_width) for a in mixed]
        + [w_out_full, inputs.reshape(rows, width), keep, gain_two[None]],
        [shape_of((rows, width), kind) for kind in (bf16, f32, bf16)],
        scratch=[vmem((count, rows, mixed_width), bf16), vmem((rows, width), f32)],
    )
    both = join(normed_two, grad_all[-1], *siblings, *gate_up[early:])
    normed_two, grad_all[-1], other_down, both = *both[:3], both[3:]
    siblings, gate_up[early:] = both[:early], both[early:]
    siblings += swap(gate_up[early:])

    gate_w, up_w, down_w = arrange(
        ids, interleaved(gate_up, siblings), w_down, other_down, width
    )
    if chips == 4:
        one, two = across(normed_two, 2), across(normed_two, 4)
        one, two, gate_w, up_w = join(one, two, gate_w, up_w)
        normed_all = [normed_two, one, two, diagonal(jnp.where(core == 0, one, two))]
    else:
        normed_all = [across(normed_two, PAIR * k) if k else normed_two for k in range(chips)]
    unit = shape_of((rows, hidden_width), bf16)
    fed = kernel_call(
        functools.partial(feed_kernel, chips),
        ids,
        [*normed_all, gate_w, up_w],
        [unit] * 3 * chips,
        vmem=32,
    )
    hidden_all, to_gate, to_up = fed[:chips], fed[chips : 2 * chips], fed[2 * chips :]

    def feed_back(at):
        outs = kernel_call(
            functools.partial(feed_back_kernel, len(at)),
            ids,
            [source[k] for source in (grad_all, to_gate, to_up) for k in at]
            + [gate_w, up_w, down_w],
            [unit, unit, shape_of((rows, width), bf16)] * len(at),
            scratch=[vmem((rows * len(at), hidden_width), bf16)] * 2,
            vmem=32,
        )
        return [list(outs[3 * i : 3 * i + 3]) for i in range(len(at))]

    down_keeps, down_sends = weight_grad(ids, hidden_all, [grad_all], PAIR, 2)
    both = join(down_sends, *grad_all)
    down_sends, grad_all = both[0], both[1:]
    down_other = across(down_sends[0, 0], 1)
    if chips == 4:
        last = feed_back([3])
        down_own = (down_keeps[0, 0].astype(f32) + down_other).astype(bf16)
        both = join(down_own, last[0][2], *grad_all)
        down_own, last[0][2], grad_all = both[0], both[1], both[2:]
        down_part = lax.psum_scatter(down_own, "ctx", scatter_dimension=0, tiled=True)
        received = [across(last[0][2], 6)]
        middles = feed_back([1, 2])
        both = join(*received, middles[0][2], middles[1][2], *grad_all)
        received, middles[0][2], middles[1][2], grad_all = both[:1], both[1], both[2], both[3:]
        received += [across(middles[0][2], 2), across(middles[1][2], 4)]
        fed = feed_back([0]) + middles + last
    else:
        fed = [feed_back([k])[0] for k in range(chips)]
        received = [across(fed[k][2], PAIR * k) for k in range(1, chips)]
        down_own = (down_keeps[0, 0].astype(f32) + down_other).astype(bf16)
        down_part = lax.psum_scatter(down_own, "ctx", scatter_dimension=0, tiled=True)
    gate_back, up_back, backs = map(list, zip(*fed))
    keeps, sends = weight_grad(ids, normed_all, [gate_back, up_back], shards)
    down_part, sends, *received = join(down_part, sends, *received)

    other = across(sends, 1)
    down_parts = [down_part, rotate(down_part, -1)]
    norm_back = kernel_call(
        functools.partial(norm_back_kernel, count, chips),
        ids,
        [backs[0], *received, middle, grad_out, keep, gain_two[None], w_out_full],
        [shape_of((rows, width), f32), shape_of((rows, width), bf16), shape_of((1, width), f32)]
        + [shape_of((rows, mixed_width), bf16)] * count,
    )
    both = join(other, *down_parts, *norm_back)
    other, down_parts, norm_back = both[0], both[1:3], both[3:]
    grad_middle, grad_branch, grad_gain_two = norm_back[:3]

    grad_parts = rotated(norm_back[3:])
    gate_up_own = [(keeps[k].astype(f32) + other[k]).astype(bf16) for k in range(chips)]
    both = join(down_part, grad_branch, *gate_up_own, *grad_parts)
    down_part, grad_branch, gate_up_own, grad_parts = *both[:2], both[2 : 2 + chips], both[2 + chips :]
    down_parts += [rotate(down_part, -step) for step in range(2, count - 1)]
    gate_up_rows = chip_exchange(gate_up_own)[:early]
    grad_parts = [a.reshape(batch, group, mixed_width) for a in grad_parts]
    grad_qkv = block_call(
        functools.partial(attend_back_kernel, count, heads, head_size),
        ids,
        qkv + grad_parts,
        qkv_width,
    )
    out_keeps, out_sends = weight_grad(ids, [mixed], [[grad_branch]], shards)
    both = join(down_part, gate_up_own[-1], out_sends, *gate_up_rows, *grad_qkv, *down_parts)
    down_part, gate_up_own[-1], out_sends, both = *both[:3], both[3:]
    gate_up_rows, grad_qkv, down_parts = both[:early], both[early:][:count], both[early + count :]
    out_other = across(out_sends[:, 0], 1)
    out_own = [(out_keeps[k, 0].astype(f32) + out_other[k]).astype(bf16) for k in range(chips)]
    gate_up_rows += chip_exchange(gate_up_own)[early:]
    grad_qkv = returned(grad_qkv)
    gate_up_sent = jnp.stack(gate_up_rows).reshape(-1, hidden_width)
    both = join(gate_up_sent, down_part, *out_own, *grad_qkv)
    gate_up_sent, down_part, out_own, grad_qkv = *both[:2], both[2 : 2 + chips], both[2 + chips :]

    gate_up_part = lax.psum_scatter(gate_up_sent, "ctx", scatter_dimension=0, tiled=True)
    down_parts += [rotate(down_part, -step) for step in range(max(2, count - 1), count)]
    out_rows = chip_exchange(out_own)[:early]
    grad_qkv, grad_gated = kernel_call(
        functools.partial(project_back_kernel, count, shards, heads),
        ids,
        [a.reshape(rows, qkv_width) for a in grad_qkv] + qkv_pieces,
        [shape_of((rows, total_width), bf16), shape_of((rows, width), f32)],
        scratch=[
            vmem((width, total_width), bf16),
            vmem((count, rows, qkv_width), bf16),
            pltpu.SemaphoreType.DMA((shards,)),
        ],
        anywhere=range(count, count + shards),
    )
    qkv_keeps, qkv_sends = weight_grad(ids, [gated], [[grad_qkv]], shards)
    both = join(qkv_sends, grad_gated, out_own[-1], down_w, *out_rows)
    qkv_sends, grad_gated, out_own[-1], down_w, out_rows = *both[:4], both[4:]
    out_rows += chip_exchange(out_own)[early:]
    ordered = [(place + step) % count for step in range(count)]
    qkv_other = across(qkv_sends[:, 0], 1)
    grad_gated = grad_gated.reshape(batch, group, width)
    grad_conv = grad_gated * gate_act
    grad_normed = grad_gated * conv_out * sig_one * (1.0 + normed * (1.0 - sig_one))
    grad_taps = [
        jnp.sum(grad_conv * normed, (0, 1)),
        jnp.sum(grad_conv * normed_ext[:, 1:-1], (0, 1)),
        jnp.sum(grad_conv * normed_ext[:, :-2], (0, 1)),
    ]
    padded = lambda a, before, after: jnp.pad(a, ((0, 0), (before, after), (0, 0)))
    grad_ext = (
        padded(taps[0] * grad_conv, 2, 0)
        + padded(taps[1] * grad_conv, 1, 1)
        + padded(taps[2] * grad_conv, 0, 2)
    )
    later_rows = along(grad_ext[:, :2], -1)
    qkv_own = [(qkv_keeps[k, 0].astype(f32) + qkv_other[k]).astype(bf16) for k in range(chips)]
    both = join(later_rows, down_w, *qkv_own, *out_rows[:early])
    later_rows, down_w, qkv_own, out_rows[:early] = *both[:2], both[2 : 2 + chips], both[2 + chips :]
    grad_normed = grad_normed + grad_ext[:, 2:] + padded(later_rows, group - 2, 0)
    residual = inputs.astype(f32)
    scale_own = scale_ext[:, 2:]
    grad_gain_one = jnp.sum(grad_normed * residual * scale_own, (0, 1))
    scaled_one = grad_normed * gain_one
    cube_one = scale_own * scale_own * scale_own
    grad_rows = (
        grad_middle.reshape(batch, group, width)
        + scale_own * scaled_one
        - residual * cube_one * jnp.mean(scaled_one * residual, -1, keepdims=True)
    ).astype(bf16)
    zero = jnp.zeros_like(grad_gain_one)
    small = jnp.stack([grad_gain_one, grad_gain_two[0]] + grad_taps + [zero, zero, zero])
    qkv_rows = chip_exchange(qkv_own)
    small = small + across(small, 1)
    out_sum = total(out_rows).astype(bf16).reshape(count, part_rows, width)
    out_parts = rotated([pick(out_sum, at) for at in ordered])

    both = join(gate_up_part, small, *down_parts, *qkv_rows, *out_parts)
    gate_up_part, small, both = both[0], both[1], both[2:]
    down_parts, qkv_rows, out_parts = both[:count], both[count:][:chips], both[count + chips :]
    gate_up_whole = lax.all_gather(gate_up_part, "ctx", axis=0, tiled=True)
    small = total([small] + [across(small, PAIR * k) for k in range(1, chips)])
    small = lax.dynamic_slice_in_dim(small, mine * own_rows, own_rows, 1)
    parts = total(qkv_rows).astype(bf16).reshape(count, part_rows, total_width)
    parts = rotated([pick(parts, at) for at in ordered])
    out_parts = returned([total(out_parts).astype(bf16)] * count)
    down_whole = placed(down_parts, ordered).reshape(w_down.shape)
    both = join(small, total(parts).astype(bf16), down_w, *hidden_all, *out_parts)
    small, part, down_w, both = *both[:3], both[3:]
    hidden_all, out_parts = both[:chips], both[chips:]
    small = total(rotated([small] * count))
    parts = returned([part] * count)
    whole = placed(parts, ordered).reshape(own_rows, total_width).astype(f32)
    grad_wout = placed(out_parts, ordered).reshape(own_rows, width).astype(f32)
    downs = kernel_call(
        functools.partial(down_kernel, chips),
        ids,
        [*hidden_all, down_w],
        [shape_of((rows, width), bf16)] * chips,
    )
    result = (middle + keep * total(chip_exchange(downs))).astype(bf16)
    gate_up_whole = gate_up_whole.reshape(chips, 2, own_rows, hidden_width)
    grad_w_gate, grad_w_up = kernel_call(
        functools.partial(finish_kernel, chips),
        ids,
        [gate_up_whole],
        [shape_of(w_gate.shape, f32)] * 2,
    )
    features = HEADS * FEAT
    return (
        result.reshape(batch, 1, group, width),
        grad_rows[:, None],
        small[0],
        small[2:5],
        whole[:, :features],
        whole[:, features : 2 * features],
        whole[:, 2 * features :],
        grad_wout,
        small[1],
        grad_w_gate,
        grad_w_up,
        down_whole.astype(f32),
    )


def solution(mesh):
    in_specs = (
        P(None, "fsdp", "ctx", None),
        P(None, "fsdp"),
        P(None, "fsdp", "ctx", None),
        P("fsdp"),
        P(None, "fsdp"),
        P("fsdp", None),
        P("fsdp", None),
        P("fsdp", None),
        P("fsdp", None),
        P("fsdp"),
        P("fsdp", None),
        P("fsdp", None),
        P("fsdp", None),
    )
    out_specs = (
        P(None, "fsdp", "ctx", None),
        P(None, "fsdp", "ctx", None),
        P("fsdp"),
        P(None, "fsdp"),
        P("fsdp", None),
        P("fsdp", None),
        P("fsdp", None),
        P("fsdp", None),
        P("fsdp"),
        P("fsdp", None),
        P("fsdp", None),
        P("fsdp", None),
    )
    return jax.shard_map(local, mesh=mesh, in_specs=in_specs, out_specs=out_specs, check_vma=False)
```

```python
import functools
import math

import jax
import jax.numpy as jnp
from jax import lax
from jax.experimental import pallas as pl
from jax.experimental.pallas import tpu as pltpu
from jax.sharding import PartitionSpec as P

HEADS = 16
FEAT = 16
PAIR = 2
FREE = pl.CostEstimate(flops=0, bytes_accessed=0, transcendentals=0)

epsilon = 1e-05
bf16 = jnp.bfloat16
f32 = jnp.float32


def dot(left, right, over):
    return lax.dot_general(left, right, (over, ((), ())), preferred_element_type=f32)


def matmul(left, right):
    return dot(left, right, ((1,), (0,)))


def left_contract(left, right):
    return dot(left, right, ((0,), (0,)))


def right_contract(left, right):
    return dot(left, right, ((1,), (1,)))


def along(value, steps):
    count = lax.axis_size("ctx")
    first, last = (max(0, -steps), min(count, count - steps))
    return lax.ppermute(value, "ctx", [(i, i + steps) for i in range(first, last)])


def rotate(value, steps):
    count = lax.axis_size("ctx")
    return lax.ppermute(value, "ctx", [(i, (i + steps) % count) for i in range(count)])


def across(value, mask):
    count = lax.axis_size("fsdp")
    return lax.ppermute(value, "fsdp", [(i, i ^ mask) for i in range(count)])


def diagonal(value):
    count = lax.axis_size("fsdp")
    return lax.ppermute(value, "fsdp", [(i, i ^ (2 if i & 1 else 4)) for i in range(count)])


def interleaved(own, other):
    return [part for pair in zip(own, other) for part in pair]


def swap(pieces):
    return [across(piece, 1) for piece in pieces]


def chip_exchange(pieces):
    return [across(p, PAIR * k) if k else p for k, p in enumerate(pieces)]


def total(pieces):
    return sum(p.astype(f32) for p in pieces[1:]) + pieces[0].astype(f32)


def join(*values):
    return list(lax.optimization_barrier(values))


def pick(stack, index):
    return lax.dynamic_index_in_dim(stack, index, 0, False)


def placed(pieces, indices):
    buffer = jnp.zeros((len(pieces),) + pieces[0].shape, pieces[0].dtype)
    for piece, index in zip(pieces, indices):
        buffer = lax.dynamic_update_index_in_dim(buffer, piece, index, 0)
    return buffer


def kernel_call(kernel, ids, arrays, outs, scratch=(), anywhere=(), vmem=24):
    whole = pl.BlockSpec(memory_space=pltpu.VMEM)
    specs = [pl.BlockSpec(memory_space=pltpu.SMEM)]
    anyplace = pl.BlockSpec(memory_space=pl.ANY)
    specs += [anyplace if i in anywhere else whole for i in range(len(arrays))]
    return pl.pallas_call(
        kernel,
        out_shape=list(outs),
        in_specs=specs,
        out_specs=[whole] * len(outs),
        scratch_shapes=list(scratch),
        compiler_params=pltpu.CompilerParams(vmem_limit_bytes=vmem * 1024 * 1024),
        cost_estimate=FREE,
    )(ids, *arrays)


def fetch_rows(pieces, whole, sems, mine):
    size = pieces[0].shape[0]
    copies = []
    for m, piece in enumerate(pieces):
        start = pl.multiple_of((mine ^ m) * size, 16)
        copies.append(pltpu.make_async_copy(piece, whole.at[pl.ds(start, size)], sems.at[m]))
    for copy in copies:
        copy.start()
    return copies


def tiles(size, step):
    return [slice(at, min(at + step, size)) for at in range(0, size, step)]


def route(value, index, refs):
    for at, ref in enumerate(refs):

        @pl.when(index == at)
        def _(ref=ref):
            ref[...] = value


def ring_step(group, place, count):
    return lax.rem(group + count - place, count)


def project_kernel(count, shards, heads, ids, gated, *rest):
    pieces, outs = rest[:shards], rest[shards : shards + count]
    weight, projected, sems = rest[shards + count :]
    place, mine = ids[0], ids[1]
    for copy in fetch_rows(pieces, weight, sems, mine):
        copy.wait()
    width = weight.shape[1]
    for tile in tiles(width, 256):
        projected[:, tile] = matmul(gated[...], weight[:, tile]).astype(bf16)
    features = heads * FEAT
    all_features = features * count
    part = (width - 2 * all_features) // count
    for group in range(count):
        start = 2 * all_features + part * group
        value = jnp.concatenate(
            [
                projected[:, features * group : features * (group + 1)],
                projected[:, all_features + features * group : all_features + features * (group + 1)],
                projected[:, start : start + part],
            ],
            -1,
        )
        route(value, ring_step(group, place, count), outs)


def project_back_kernel(count, shards, heads, ids, *rest):
    ins, pieces = rest[:count], rest[count : count + shards]
    natural, grad = rest[count + shards : count + shards + 2]
    weight, grouped, sems = rest[count + shards + 2 :]
    place, mine = ids[0], ids[1]
    copies = fetch_rows(pieces, weight, sems, mine)
    features = heads * FEAT
    part = ins[0].shape[1] - 2 * features
    for step in range(count):
        grouped[lax.rem(place + step, count)] = ins[step][...]
    parts = [grouped[g, :, :features] for g in range(count)]
    parts += [grouped[g, :, features : 2 * features] for g in range(count)]
    parts += [grouped[g, :, 2 * features :] for g in range(count)]
    natural[...] = jnp.concatenate(parts, -1)
    for copy in copies:
        copy.wait()
    for tile in tiles(weight.shape[0], 256):
        grad[:, tile] = right_contract(natural[...], weight[tile])


def merge_kernel(count, ids, *rest):
    ins = rest[:count]
    weight, inputs, keep, gain, mixed, middle, normed, grouped, branch = rest[count:]
    place = ids[0]
    for step in range(count):
        grouped[lax.rem(place + step, count)] = ins[step][...]
    mixed[...] = jnp.concatenate([grouped[g] for g in range(count)], -1)
    for tile in tiles(weight.shape[1], 256):
        branch[:, tile] = matmul(mixed[...], weight[:, tile])

    @pl.loop(0, inputs.shape[0] // 16)
    def _(i):
        rows = pl.ds(pl.multiple_of(i * 16, 16), 16)
        value = inputs[rows].astype(f32) + keep[rows] * branch[rows]
        middle[rows] = value
        scale = lax.rsqrt(jnp.mean(value * value, -1, keepdims=True) + epsilon)
        normed[rows] = (value * scale * gain[...]).astype(bf16)


def norm_back_kernel(count, chips, ids, *rest):
    backs = rest[:chips]
    middle, grad_out, keep, gain, weight = rest[chips : chips + 5]
    grad_middle, grad_branch, grad_gain = rest[chips + 5 : chips + 8]
    outs = rest[chips + 8 :]
    place = ids[0]
    grad_gain[...] = jnp.zeros_like(grad_gain)

    @pl.loop(0, middle.shape[0] // 16)
    def _(i):
        rows = pl.ds(pl.multiple_of(i * 16, 16), 16)
        back = backs[0][rows].astype(f32)
        for ref in backs[1:]:
            back = back + ref[rows].astype(f32)
        value = middle[rows]
        scale = lax.rsqrt(jnp.mean(value * value, -1, keepdims=True) + epsilon)
        grad_gain[...] += jnp.sum(back * value * scale, 0, keepdims=True)
        scaled = back * gain[...]
        cube = scale * scale * scale
        grad = (
            grad_out[rows].astype(f32)
            + scale * scaled
            - value * (cube * jnp.mean(scaled * value, -1, keepdims=True))
        )
        grad_middle[rows] = grad
        grad_branch[rows] = (keep[rows] * grad).astype(bf16)

    part = weight.shape[0] // count
    for group in range(count):
        value = right_contract(grad_branch[...], weight[group * part : (group + 1) * part])
        route(value.astype(bf16), ring_step(group, place, count), outs)


def arrange_kernel(shards, ids, *rest):
    pieces, own_down, other_down = rest[:shards], rest[shards], rest[shards + 1]
    gate, up, down, sems = rest[shards + 2 :]
    mine = ids[1]
    size = pieces[0].shape[1]
    copies = []
    for m, piece in enumerate(pieces):
        rows = pl.ds(pl.multiple_of((mine ^ m) * size, 16), size)
        for half, out in enumerate((gate, up)):
            copies.append(pltpu.make_async_copy(piece.at[half], out.at[rows], sems.at[2 * m + half]))
    size = own_down.shape[0]
    core = lax.rem(mine, PAIR)
    for at, piece in enumerate((own_down, other_down)):
        rows = pl.ds(pl.multiple_of((core ^ at) * size, 16), size)
        copies.append(pltpu.make_async_copy(piece, down.at[rows], sems.at[2 * shards + at]))
    for copy in copies:
        copy.start()
    for copy in copies:
        copy.wait()


def pack_kernel(chips, ids, gate, up, out):
    chip = lax.div(ids[1], PAIR)
    part = gate.shape[1] // chips
    for q in range(chips):
        for half, ref in enumerate((gate, up)):
            out[q ^ chip, half] = ref[:, q * part : (q + 1) * part]


def feed_kernel(chunks, ids, *rest):
    tokens = jnp.concatenate([ref[...] for ref in rest[:chunks]], 0)
    gate_w, up_w = rest[chunks : chunks + 2]
    hidden, to_gate, to_up = (rest[chunks + 2 + i * chunks :][:chunks] for i in range(3))
    size = tokens.shape[0] // chunks

    def put(refs, tile, value):
        for k, ref in enumerate(refs):
            ref[:, tile] = value[k * size : (k + 1) * size].astype(bf16)

    for tile in tiles(gate_w.shape[1], 256):
        gate_pre = matmul(tokens, gate_w[:, tile])
        up_pre = matmul(tokens, up_w[:, tile])
        sig = jax.nn.sigmoid(gate_pre)
        gate_silu = gate_pre * sig
        put(hidden, tile, gate_silu * up_pre)
        put(to_gate, tile, up_pre * sig * (1.0 + gate_pre * (1.0 - sig)))
        put(to_up, tile, gate_silu)


def feed_back_kernel(chunks, ids, *rest):
    grad_out = jnp.concatenate([ref[...] for ref in rest[:chunks]], 0)
    to_gate = jnp.concatenate([ref[...] for ref in rest[chunks : 2 * chunks]], 0)
    to_up = jnp.concatenate([ref[...] for ref in rest[2 * chunks : 3 * chunks]], 0)
    gate_w, up_w, down_w = rest[3 * chunks : 3 * chunks + 3]
    outs = rest[3 * chunks + 3 : -2]
    gate_all, up_all = rest[-2:]
    size = grad_out.shape[0] // chunks

    def put(which, tile, value):
        for k in range(chunks):
            outs[3 * k + which][:, tile] = value[k * size : (k + 1) * size].astype(bf16)

    for tile in tiles(gate_w.shape[1], 256):
        grad_hidden = right_contract(grad_out, down_w[tile])
        gate_back = (grad_hidden * to_gate[:, tile].astype(f32)).astype(bf16)
        up_back = (grad_hidden * to_up[:, tile].astype(f32)).astype(bf16)
        gate_all[:, tile], up_all[:, tile] = gate_back, up_back
        put(0, tile, gate_back)
        put(1, tile, up_back)
    for tile in tiles(gate_w.shape[0], 256):
        value = right_contract(gate_all[...], gate_w[tile])
        put(2, tile, value + right_contract(up_all[...], up_w[tile]))


def down_kernel(chips, ids, *rest):
    hidden, weight, outs = rest[:chips], rest[chips], rest[chips + 1 :]
    for tile in tiles(weight.shape[1], 256):
        for source, out in zip(hidden, outs):
            out[:, tile] = matmul(source[...], weight[:, tile]).astype(bf16)


def finish_kernel(chips, ids, whole, gate, up):
    chip = lax.div(ids[1], PAIR)
    part = whole.shape[-1]
    for q in range(chips):
        for half, out in enumerate((gate, up)):
            out[:, q * part : (q + 1) * part] = whole[q ^ chip, half].astype(f32)


def weight_grad_kernel(blocks, groups, parts, ids, *rest):
    chunks = (len(rest) - 3) // (groups + 1)
    lefts, rights = rest[:chunks], rest[chunks:-3]
    keeps, sends, turned = rest[-3:]
    mine = lax.rem(ids[1], blocks)
    tokens, rows = lefts[0].shape
    size = rows // blocks
    step = size // parts

    @pl.when((pl.program_id(0) == 0) & (pl.program_id(1) == 0) & (pl.program_id(2) == 0))
    def _():
        for k, left in enumerate(lefts):
            for tile in tiles(rows, 128):
                turned[tile, k * tokens : (k + 1) * tokens] = left[:, tile].T

    for g in range(groups):

        @pl.when(pl.program_id(0) == g)
        def _(g=g):
            right = [part[...] for part in rights[g * chunks : (g + 1) * chunks]]
            right = jnp.concatenate(right, 0)
            for at, out in enumerate((keeps, sends)):
                block = mine ^ (PAIR * pl.program_id(1) + at)
                start = pl.multiple_of(block * size + pl.program_id(2) * step, 16)
                out[0, 0] = matmul(turned[pl.ds(start, step)], right).astype(bf16)


def weight_grad(ids, lefts, rights, blocks, parts=1):
    groups, chunks = len(rights), len(lefts)
    tokens, rows = lefts[0].shape
    columns = rights[0][0].shape[1]
    size = rows // blocks
    out = jax.ShapeDtypeStruct((blocks // PAIR, groups, size, columns), bf16)
    arrays = list(lefts) + [part for right in rights for part in right]
    block = pl.BlockSpec((1, 1, size // parts, columns), lambda g, k, j: (k, g, j, 0))
    return pl.pallas_call(
        functools.partial(weight_grad_kernel, blocks, groups, parts),
        out_shape=[out, out],
        grid=(groups, blocks // PAIR, parts),
        in_specs=[pl.BlockSpec(memory_space=pltpu.SMEM)]
        + [pl.BlockSpec(memory_space=pltpu.VMEM)] * len(arrays),
        out_specs=[block] * 2,
        scratch_shapes=[pltpu.VMEM((rows, chunks * tokens), bf16)],
        compiler_params=pltpu.CompilerParams(vmem_limit_bytes=24 * 1024 * 1024),
        cost_estimate=FREE,
    )(ids, *arrays)


def pack_call(ids, w_gate, w_up, chips):
    rows, columns = w_gate.shape
    out = jax.ShapeDtypeStruct((chips, 2, rows, columns // chips), bf16)
    return kernel_call(functools.partial(pack_kernel, chips), ids, [w_gate, w_up], [out])


def arrange(ids, pieces, own_down, other_down, width):
    shards = len(pieces)
    hidden_width = pieces[0].shape[-1]
    shape_of = jax.ShapeDtypeStruct
    anywhere = pl.BlockSpec(memory_space=pl.ANY)
    return pl.pallas_call(
        functools.partial(arrange_kernel, shards),
        out_shape=[shape_of((width, hidden_width), bf16)] * 2
        + [shape_of((PAIR * own_down.shape[0], width), bf16)],
        in_specs=[pl.BlockSpec(memory_space=pltpu.SMEM)] + [anywhere] * (shards + 2),
        out_specs=[pl.BlockSpec(memory_space=pltpu.VMEM)] * 3,
        scratch_shapes=[pltpu.SemaphoreType.DMA((2 * shards + 2,))],
        compiler_params=pltpu.CompilerParams(vmem_limit_bytes=24 * 1024 * 1024),
        cost_estimate=FREE,
    )(ids, *pieces, own_down, other_down)


def causal(place, count, group, block):
    row_block = lax.rem(place + (count - block), count)
    rows = row_block * group + lax.broadcasted_iota(jnp.int32, (group, count * group), 0)
    column = lax.broadcasted_iota(jnp.int32, (group, count * group), 1)
    ordinal, inner = column // group, column % group
    columns = lax.rem(place + (count - ordinal), count) * group + inner
    return rows >= columns


def head_parts(refs, head, heads, head_size):
    features = heads * FEAT
    queries = [r[0][:, head * FEAT : (head + 1) * FEAT] * 0.25 for r in refs]
    keys = [r[0][:, features + head * FEAT : features + (head + 1) * FEAT] for r in refs]
    start = 2 * features + head * head_size
    values = [r[0][:, start : start + head_size] for r in refs]
    return queries, jnp.concatenate(keys, 0), jnp.concatenate(values, 0)


def attend_kernel(count, heads, head_size, place_ref, *refs):
    ins, outs = refs[:count], refs[count:]
    group = ins[0].shape[1]
    place = place_ref[0]
    masks = [causal(place, count, group, block) for block in range(count)]
    mixed = [[] for _ in range(count)]
    for head in range(heads):
        queries, keys, values = head_parts(ins, head, heads, head_size)
        for block in range(count):
            scores = right_contract(queries[block], keys)
            weights = jnp.where(masks[block], 1.0 + scores + 0.5 * scores * scores, 0.0)
            denominator = jnp.sum(weights, -1, keepdims=True)
            numerator = matmul(weights.astype(bf16), values)
            mixed[block].append((numerator / denominator).astype(bf16))
    for block in range(count):
        outs[block][0] = jnp.concatenate(mixed[block], -1)


def attend_back_kernel(count, heads, head_size, place_ref, *refs):
    ins, grads, outs = refs[:count], refs[count : 2 * count], refs[2 * count :]
    group = ins[0].shape[1]
    place = place_ref[0]
    masks = [causal(place, count, group, block) for block in range(count)]
    dqs = [[] for _ in range(count)]
    dks, dvs = [], []
    for head in range(heads):
        queries, keys, values = head_parts(ins, head, heads, head_size)
        key_back = value_back = 0.0
        for block in range(count):
            upstream = grads[block][0][:, head * head_size : (head + 1) * head_size]
            scores = right_contract(queries[block], keys)
            weights = jnp.where(masks[block], 1.0 + scores + 0.5 * scores * scores, 0.0)
            inverse = 1.0 / jnp.sum(weights, -1, keepdims=True)
            weights = weights * inverse
            inner = right_contract(upstream, values)
            shift = jnp.sum(weights * inner, -1, keepdims=True)
            score_back = (inner - shift) * inverse * (1.0 + scores)
            score_back = jnp.where(masks[block], score_back, 0.0).astype(bf16)
            dqs[block].append((0.25 * matmul(score_back, keys)).astype(bf16))
            key_back = key_back + left_contract(queries[block], score_back)
            value_back = value_back + left_contract(upstream, weights.astype(bf16))
        dks.append(key_back.T.astype(bf16))
        dvs.append(value_back.T.astype(bf16))
    for block in range(count):
        rows = slice(block * group, (block + 1) * group)
        parts = dqs[block] + [k[rows] for k in dks] + [v[rows] for v in dvs]
        outs[block][0] = jnp.concatenate(parts, -1)


def block_call(kernel, ids, arrays, out_width):
    count = lax.axis_size("ctx")
    batch, group, _ = arrays[0].shape
    spec = lambda a: pl.BlockSpec((1, group, a.shape[2]), lambda b: (b, 0, 0))
    out = jax.ShapeDtypeStruct((batch, group, out_width), bf16)
    return pl.pallas_call(
        kernel,
        out_shape=[out] * count,
        grid=(batch,),
        in_specs=[pl.BlockSpec(memory_space=pltpu.SMEM)] + [spec(a) for a in arrays],
        out_specs=[spec(out)] * count,
        compiler_params=pltpu.CompilerParams(vmem_limit_bytes=24 * 1024 * 1024),
        cost_estimate=FREE,
    )(ids, *arrays)


def local(
    block_input,
    lengths,
    cotangent,
    gain_attn,
    conv_taps,
    w_query,
    w_key,
    w_value,
    w_out,
    gain_ffn,
    w_gate,
    w_up,
    w_down,
):
    count = lax.axis_size("ctx")
    shards = lax.axis_size("fsdp")
    chips = shards // PAIR
    place = lax.axis_index("ctx")
    mine = lax.axis_index("fsdp")
    core, chip = mine % PAIR, mine // PAIR
    ids = jnp.stack([place, mine]).astype(jnp.int32)
    batch, _, group, width = block_input.shape
    rows = batch * group
    own_rows = w_query.shape[0]
    heads = HEADS // count
    head_size = width // HEADS
    mixed_width = heads * head_size
    qkv_width = 2 * heads * FEAT + mixed_width
    hidden_width = w_gate.shape[1] // chips
    part_rows = own_rows // count
    vmem = lambda shape, kind: pltpu.VMEM(shape, kind)
    shape_of = jax.ShapeDtypeStruct
    rotated = lambda pieces: [rotate(p, d) if d else p for d, p in enumerate(pieces)]
    returned = lambda pieces: [rotate(p, -d) if d else p for d, p in enumerate(pieces)]

    small = jnp.concatenate([gain_attn[None], gain_ffn[None], conv_taps], 0)
    small = jnp.pad(small, ((0, 3), (0, 0)))[None]
    mask = 1
    while mask < shards:
        small = jnp.concatenate([small, across(small, mask)], 0)
        mask *= 2
    small = placed([small[m] for m in range(shards)], [mine ^ m for m in range(shards)])
    small = jnp.transpose(small, (1, 0, 2)).reshape(8, width).astype(f32)
    gain_one, gain_two, taps = small[0], small[1], small[2:5]
    inputs = block_input[:, 0]
    previous = along(inputs[:, group - 2 :], 1)

    qkv_shard = jnp.concatenate([w_query, w_key, w_value], -1)
    total_width = qkv_shard.shape[1]
    if chips == 4:
        one, two = across(qkv_shard, 2), across(qkv_shard, 4)
        (packed,) = pack_call(ids, w_gate, w_up, chips)
        one, two, packed = join(one, two, packed)
        three = diagonal(jnp.where(core == 0, one, two))
        others = swap([qkv_shard, one, two])
        three, *others = join(three, *others)
        qkv_own, qkv_other = [qkv_shard, one, two, three], others + swap([three])
    else:
        (packed,) = pack_call(ids, w_gate, w_up, chips)
        qkv_own = join(*[across(qkv_shard, PAIR * k) if k else qkv_shard for k in range(chips)])
        qkv_other = swap(qkv_own)

    extended = jnp.concatenate([previous, inputs], 1).astype(f32)
    scale_ext = lax.rsqrt(jnp.mean(extended * extended, -1, keepdims=True) + epsilon)
    normed_ext = extended * scale_ext * gain_one
    normed = normed_ext[:, 2:]
    conv_out = taps[0] * normed + taps[1] * normed_ext[:, 1:-1] + taps[2] * normed_ext[:, :-2]
    sig_one = jax.nn.sigmoid(normed)
    gate_act = normed * sig_one
    gated = (conv_out * gate_act).astype(bf16).reshape(rows, width)
    positions = place * group + lax.iota(jnp.int32, group)
    keep = (positions[None] < lengths).astype(f32).reshape(rows, 1)
    grad_out = (cotangent[:, 0].astype(f32).reshape(rows, width) * keep).astype(bf16)

    gated, w_out, w_down, packed, grad_out, *qkv_other = join(
        gated, w_out, w_down, packed, grad_out, *qkv_other
    )
    qkv_pieces = interleaved(qkv_own, qkv_other)
    w_out_full = lax.all_gather(w_out, "fsdp", axis=0, tiled=True)
    if chips == 4:
        grad_all = [grad_out, across(grad_out, 2), across(grad_out, 4)]
    else:
        grad_all = [across(grad_out, PAIR * k) if k else grad_out for k in range(chips)]

    projected = kernel_call(
        functools.partial(project_kernel, count, shards, heads),
        ids,
        [gated] + qkv_pieces,
        [shape_of((rows, qkv_width), bf16)] * count,
        scratch=[
            vmem((width, total_width), bf16),
            vmem((rows, total_width), bf16),
            pltpu.SemaphoreType.DMA((shards,)),
        ],
        anywhere=range(1, shards + 1),
    )
    packed, *projected = join(packed, *projected)
    early = max(1, chips - 1)
    gate_up = [across(packed[k], PAIR * k) if k else packed[0] for k in range(early)]
    qkv = rotated(projected)
    both = join(*qkv, *grad_all)
    qkv, grad_all = both[:count], both[count:]
    qkv = [a.reshape(batch, group, qkv_width) for a in qkv]
    mixed = block_call(
        functools.partial(attend_kernel, count, heads, head_size), ids, qkv, mixed_width
    )
    *mixed, packed = join(*mixed, packed)
    mixed = returned(mixed)
    relayed = jnp.where(core == 0, grad_all[1], grad_all[2]) if chips == 4 else grad_all.pop()
    both = join(w_down, packed, relayed, *gate_up[:early], *mixed)
    own_down, packed, relayed, gate_up, mixed = *both[:3], both[3 : 3 + early], both[3 + early :]
    grad_all.append(diagonal(relayed) if chips == 4 else relayed)
    siblings = swap([own_down, *gate_up])
    gate_up += [across(packed[k], PAIR * k) for k in range(early, chips)]
    mixed, middle, normed_two = kernel_call(
        functools.partial(merge_kernel, count),
        ids,
        [a.reshape(rows, mixed_width) for a in mixed]
        + [w_out_full, inputs.reshape(rows, width), keep, gain_two[None]],
        [shape_of((rows, width), kind) for kind in (bf16, f32, bf16)],
        scratch=[vmem((count, rows, mixed_width), bf16), vmem((rows, width), f32)],
    )
    both = join(normed_two, grad_all[-1], *siblings, *gate_up[early:])
    normed_two, grad_all[-1], other_down, both = *both[:3], both[3:]
    siblings, gate_up[early:] = both[:early], both[early:]
    siblings += swap(gate_up[early:])

    gate_w, up_w, down_w = arrange(
        ids, interleaved(gate_up, siblings), w_down, other_down, width
    )
    if chips == 4:
        one, two = across(normed_two, 2), across(normed_two, 4)
        one, two, gate_w, up_w = join(one, two, gate_w, up_w)
        normed_all = [normed_two, one, two, diagonal(jnp.where(core == 0, one, two))]
    else:
        normed_all = [across(normed_two, PAIR * k) if k else normed_two for k in range(chips)]
    unit = shape_of((rows, hidden_width), bf16)
    fed = kernel_call(
        functools.partial(feed_kernel, chips),
        ids,
        [*normed_all, gate_w, up_w],
        [unit] * 3 * chips,
        vmem=28,
    )
    hidden_all, to_gate, to_up = fed[:chips], fed[chips : 2 * chips], fed[2 * chips :]

    def feed_back(at):
        outs = kernel_call(
            functools.partial(feed_back_kernel, len(at)),
            ids,
            [source[k] for source in (grad_all, to_gate, to_up) for k in at]
            + [gate_w, up_w, down_w],
            [unit, unit, shape_of((rows, width), bf16)] * len(at),
            scratch=[vmem((rows * len(at), hidden_width), bf16)] * 2,
            vmem=24,
        )
        return [list(outs[3 * i : 3 * i + 3]) for i in range(len(at))]

    down_keeps, down_sends = weight_grad(ids, hidden_all, [grad_all], PAIR, 2)
    both = join(down_sends, *grad_all)
    down_sends, grad_all = both[0], both[1:]
    down_other = across(down_sends[0, 0], 1)
    if chips == 4:
        last = feed_back([3])
        down_own = (down_keeps[0, 0].astype(f32) + down_other).astype(bf16)
        both = join(down_own, last[0][2], *grad_all)
        down_own, last[0][2], grad_all = both[0], both[1], both[2:]
        down_part = lax.psum_scatter(down_own, "ctx", scatter_dimension=0, tiled=True)
        received = [across(last[0][2], 6)]
        middles = feed_back([1, 2])
        both = join(*received, middles[0][2], middles[1][2], *grad_all)
        received, middles[0][2], middles[1][2], grad_all = both[:1], both[1], both[2], both[3:]
        received += [across(middles[0][2], 2), across(middles[1][2], 4)]
        fed = feed_back([0]) + middles + last
    else:
        fed = [feed_back([k])[0] for k in range(chips)]
        received = [across(fed[k][2], PAIR * k) for k in range(1, chips)]
        down_own = (down_keeps[0, 0].astype(f32) + down_other).astype(bf16)
        down_part = lax.psum_scatter(down_own, "ctx", scatter_dimension=0, tiled=True)
    gate_back, up_back, backs = map(list, zip(*fed))
    keeps, sends = weight_grad(ids, normed_all, [gate_back, up_back], shards)
    down_part, sends, *received = join(down_part, sends, *received)

    other = across(sends, 1)
    down_parts = [down_part, rotate(down_part, -1)]
    norm_back = kernel_call(
        functools.partial(norm_back_kernel, count, chips),
        ids,
        [backs[0], *received, middle, grad_out, keep, gain_two[None], w_out_full],
        [shape_of((rows, width), f32), shape_of((rows, width), bf16), shape_of((1, width), f32)]
        + [shape_of((rows, mixed_width), bf16)] * count,
    )
    both = join(other, *down_parts, *norm_back)
    other, down_parts, norm_back = both[0], both[1:3], both[3:]
    grad_middle, grad_branch, grad_gain_two = norm_back[:3]

    grad_parts = rotated(norm_back[3:])
    gate_up_own = [(keeps[k].astype(f32) + other[k]).astype(bf16) for k in range(chips)]
    both = join(down_part, grad_branch, *gate_up_own, *grad_parts)
    down_part, grad_branch, gate_up_own, grad_parts = *both[:2], both[2 : 2 + chips], both[2 + chips :]
    down_parts += [rotate(down_part, -step) for step in range(2, count - 1)]
    gate_up_rows = chip_exchange(gate_up_own)[:early]
    grad_parts = [a.reshape(batch, group, mixed_width) for a in grad_parts]
    grad_qkv = block_call(
        functools.partial(attend_back_kernel, count, heads, head_size),
        ids,
        qkv + grad_parts,
        qkv_width,
    )
    out_keeps, out_sends = weight_grad(ids, [mixed], [[grad_branch]], shards)
    both = join(down_part, gate_up_own[-1], out_sends, *gate_up_rows, *grad_qkv, *down_parts)
    down_part, gate_up_own[-1], out_sends, both = *both[:3], both[3:]
    gate_up_rows, grad_qkv, down_parts = both[:early], both[early:][:count], both[early + count :]
    out_other = across(out_sends[:, 0], 1)
    out_own = [(out_keeps[k, 0].astype(f32) + out_other[k]).astype(bf16) for k in range(chips)]
    gate_up_rows += chip_exchange(gate_up_own)[early:]
    grad_qkv = returned(grad_qkv)
    gate_up_sent = jnp.stack(gate_up_rows).reshape(-1, hidden_width)
    both = join(down_part, *out_own, *grad_qkv)
    down_part, out_own, grad_qkv = both[0], both[1 : 1 + chips], both[1 + chips :]

    gate_up_part = lax.psum_scatter(gate_up_sent, "ctx", scatter_dimension=0, tiled=True)
    down_parts += [rotate(down_part, -step) for step in range(max(2, count - 1), count)]
    out_rows = chip_exchange(out_own)[:early]
    grad_qkv, grad_gated = kernel_call(
        functools.partial(project_back_kernel, count, shards, heads),
        ids,
        [a.reshape(rows, qkv_width) for a in grad_qkv] + qkv_pieces,
        [shape_of((rows, total_width), bf16), shape_of((rows, width), f32)],
        scratch=[
            vmem((width, total_width), bf16),
            vmem((count, rows, qkv_width), bf16),
            pltpu.SemaphoreType.DMA((shards,)),
        ],
        anywhere=range(count, count + shards),
    )
    qkv_keeps, qkv_sends = weight_grad(ids, [gated], [[grad_qkv]], shards)
    both = join(qkv_sends, grad_gated, out_own[-1], down_w, *out_rows)
    qkv_sends, grad_gated, out_own[-1], down_w, out_rows = *both[:4], both[4:]
    out_rows += chip_exchange(out_own)[early:]
    ordered = [(place + step) % count for step in range(count)]
    qkv_other = across(qkv_sends[:, 0], 1)
    grad_gated = grad_gated.reshape(batch, group, width)
    grad_conv = grad_gated * gate_act
    grad_normed = grad_gated * conv_out * sig_one * (1.0 + normed * (1.0 - sig_one))
    grad_taps = [
        jnp.sum(grad_conv * normed, (0, 1)),
        jnp.sum(grad_conv * normed_ext[:, 1:-1], (0, 1)),
        jnp.sum(grad_conv * normed_ext[:, :-2], (0, 1)),
    ]
    padded = lambda a, before, after: jnp.pad(a, ((0, 0), (before, after), (0, 0)))
    grad_ext = (
        padded(taps[0] * grad_conv, 2, 0)
        + padded(taps[1] * grad_conv, 1, 1)
        + padded(taps[2] * grad_conv, 0, 2)
    )
    later_rows = along(grad_ext[:, :2], -1)
    qkv_own = [(qkv_keeps[k, 0].astype(f32) + qkv_other[k]).astype(bf16) for k in range(chips)]
    both = join(later_rows, down_w, *qkv_own, *out_rows[:early])
    later_rows, down_w, qkv_own, out_rows[:early] = *both[:2], both[2 : 2 + chips], both[2 + chips :]
    grad_normed = grad_normed + grad_ext[:, 2:] + padded(later_rows, group - 2, 0)
    residual = inputs.astype(f32)
    scale_own = scale_ext[:, 2:]
    grad_gain_one = jnp.sum(grad_normed * residual * scale_own, (0, 1))
    scaled_one = grad_normed * gain_one
    cube_one = scale_own * scale_own * scale_own
    grad_rows = (
        grad_middle.reshape(batch, group, width)
        + scale_own * scaled_one
        - residual * cube_one * jnp.mean(scaled_one * residual, -1, keepdims=True)
    ).astype(bf16)
    zero = jnp.zeros_like(grad_gain_one)
    small = jnp.stack([grad_gain_one, grad_gain_two[0]] + grad_taps + [zero, zero, zero])
    qkv_rows = chip_exchange(qkv_own)
    small = small + across(small, 1)
    out_sum = total(out_rows).astype(bf16).reshape(count, part_rows, width)
    out_parts = rotated([pick(out_sum, at) for at in ordered])

    both = join(gate_up_part, small, *down_parts, *qkv_rows, *out_parts)
    gate_up_part, small, both = both[0], both[1], both[2:]
    down_parts, qkv_rows, out_parts = both[:count], both[count:][:chips], both[count + chips :]
    gate_up_whole = lax.all_gather(gate_up_part, "ctx", axis=0, tiled=True)
    small = total([small] + [across(small, PAIR * k) for k in range(1, chips)])
    small = lax.dynamic_slice_in_dim(small, mine * own_rows, own_rows, 1)
    parts = total(qkv_rows).astype(bf16).reshape(count, part_rows, total_width)
    parts = rotated([pick(parts, at) for at in ordered])
    out_parts = returned([total(out_parts).astype(bf16)] * count)
    down_whole = placed(down_parts, ordered).reshape(w_down.shape)
    both = join(small, total(parts).astype(bf16), down_w, *hidden_all, *out_parts)
    small, part, down_w, both = *both[:3], both[3:]
    hidden_all, out_parts = both[:chips], both[chips:]
    small = total(rotated([small] * count))
    parts = returned([part] * count)
    whole = placed(parts, ordered).reshape(own_rows, total_width).astype(f32)
    grad_wout = placed(out_parts, ordered).reshape(own_rows, width).astype(f32)
    downs = kernel_call(
        functools.partial(down_kernel, chips),
        ids,
        [*hidden_all, down_w],
        [shape_of((rows, width), bf16)] * chips,
    )
    result = (middle + keep * total(chip_exchange(downs))).astype(bf16)
    gate_up_whole = gate_up_whole.reshape(chips, 2, own_rows, hidden_width)
    grad_w_gate, grad_w_up = kernel_call(
        functools.partial(finish_kernel, chips),
        ids,
        [gate_up_whole],
        [shape_of(w_gate.shape, f32)] * 2,
    )
    features = HEADS * FEAT
    return (
        result.reshape(batch, 1, group, width),
        grad_rows[:, None],
        small[0],
        small[2:5],
        whole[:, :features],
        whole[:, features : 2 * features],
        whole[:, 2 * features :],
        grad_wout,
        small[1],
        grad_w_gate,
        grad_w_up,
        down_whole.astype(f32),
    )


def solution(mesh):
    in_specs = (
        P(None, "fsdp", "ctx", None),
        P(None, "fsdp"),
        P(None, "fsdp", "ctx", None),
        P("fsdp"),
        P(None, "fsdp"),
        P("fsdp", None),
        P("fsdp", None),
        P("fsdp", None),
        P("fsdp", None),
        P("fsdp"),
        P("fsdp", None),
        P("fsdp", None),
        P("fsdp", None),
    )
    out_specs = (
        P(None, "fsdp", "ctx", None),
        P(None, "fsdp", "ctx", None),
        P("fsdp"),
        P(None, "fsdp"),
        P("fsdp", None),
        P("fsdp", None),
        P("fsdp", None),
        P("fsdp", None),
        P("fsdp"),
        P("fsdp", None),
        P("fsdp", None),
        P("fsdp", None),
    )
    return jax.shard_map(local, mesh=mesh, in_specs=in_specs, out_specs=out_specs, check_vma=False)
```
